32 devices in a mesh: grp: 2 (over x), inst: 8 (over z, y), tp: 2 (over core).
Axes of the slice: x: 2, y: 2, z: 4, core: 2. Of those that a mesh axis runs over, the one named last changes fastest.
Arguments:
- tokens: bfloat16 [2, 2560, 4096], P(None, ('grp', 'inst'), 'tp'), parts along dimension 1, may hold values from -6 to 6
- queries: bfloat16 [2, 2560, 8192], P(None, ('grp', 'inst'), 'tp'), parts along dimension 1, may hold values from -100 to 100
- key_value_cache: bfloat16 [2560, 8, 2, 1024], P(('grp', 'inst'), None, None, 'tp'), parts along dimension 0, may hold values from -4 to 4
- key_value_length: int32 [2560], P(('grp', 'inst')), parts along dimension 0, may hold values from 2 to 8, as said below
- request_adapter_index: int32 [2560, 1], P(('grp', 'inst')), parts along dimension 0, may hold values from 0 to 7; in each aligned block of 160 rows (0 to 159, 160 to 319, ...) at most 24 rows name the same one
- adapter_destination: int32 [128], P('grp'), parts along dimension 0, may hold values from 0 to 7, as said below
- key_matrix: bfloat16 [4096, 1024], P('tp'), may hold values from -0.09375 to 0.09375
- value_matrix: bfloat16 [4096, 1024], P('tp'), may hold values from -0.09375 to 0.09375
- adapter_down_maps: bfloat16 [128, 4096, 128], P(('grp', 'inst'), 'tp'), parts along dimension 0, may hold values from -0.09375 to 0.09375
- adapter_up_maps: bfloat16 [128, 2, 64, 1024], P(('grp', 'inst'), None, None, 'tp'), parts along dimension 0, may hold values from -0.75 to 0.75
Outputs:
- attended: bfloat16 [2, 3072, 8192], P(None, ('grp', 'inst'), 'tp'), parts along dimension 1
- new_kv: bfloat16 [2, 3072, 2, 1024], P(None, ('grp', 'inst'), None, 'tp'), parts along dimension 1
The draws below stay inside these ranges and needn't reach their ends.
There are 2 independent parts, one for each index of `grp`. The reference program is written for one: setup_inputs(seed, part) draws one part's arguments, and reference() takes and returns one part's arrays. A program takes and returns all parts, laid end to end along the dimension named above; an argument that names none is the same for every part. Nothing has to cross between parts.
Inputs may be any that keep to these rules, and one draw needn't show every extreme that they name: `adapter_destination`: each instance is the destination of exactly 8 adapters, at most one of them from any one instance (its own included). `key_value_length`: every instance holds a request with exactly 8 live positions. `request_adapter_index`: among one instance's 160 requests at most 24 use the same adapter, and some adapter has exactly 24.
All inputs are finite; a program needn't handle non-finite values.
Results may differ from the reference program's by a relative error of at most 0.0065.
Values may be sent and summed in bfloat16 or wider, within the bound.
A program may use at most 192 MiB of HBM per device.

```python
import math
import jax
import jax.numpy as jnp
import numpy as np
from jax import lax

FEATURES_IN = 4096
KEY_VALUE_HEADS = 8
QUERY_GROUP = 8
HEAD_SIZE = 128
ADAPTER_RANK = 64
DECODE_STEPS = 2
ADAPTERS_START = 8
SEG = 24
R_INST = 160
CONTEXT_LENGTH = 8
KEY_VALUE_WIDTH = 1024
HQW = 8192
ADAPTER_COUNT = 64
REQUEST_ROWS = 1280
DROWS = 1536
N_INST = 8


def cache_field(key):
    return jax.random.truncated_normal(key, -4.0, 4.0, (REQUEST_ROWS, CONTEXT_LENGTH, 2, KEY_VALUE_WIDTH), jnp.float32)


def draw_key_value_cache(key, part):
    cached_state = cache_field(key)
    return cached_state.astype(jnp.bfloat16)


def draw_queries(key, part):
    key = jax.random.fold_in(key, 5)
    first_key = jax.random.fold_in(key, 0)
    result = jax.random.truncated_normal(first_key, -6.0, 6.0, (DECODE_STEPS, REQUEST_ROWS, HQW), jnp.float32)
    return result.astype(jnp.bfloat16)


def draw_key_value_length(key, part):
    key = jax.random.fold_in(key, 7)
    first_key, second_key = jax.random.split(key, 2)
    lengths = jax.random.randint(first_key, (REQUEST_ROWS,), 2, CONTEXT_LENGTH + 1)
    longest = jax.random.randint(second_key, (REQUEST_ROWS // R_INST,), 0, R_INST)
    marked = jnp.arange(REQUEST_ROWS) % R_INST == jnp.repeat(longest, R_INST)
    return jnp.where(marked, CONTEXT_LENGTH, lengths).astype(jnp.int32)


def draw_adapter_destination(key, part):
    key = jax.random.fold_in(key, 11)
    first_key, second_key, third_key = jax.random.split(key, 3)
    instances = ADAPTER_COUNT // ADAPTERS_START
    sigma_order = jax.random.permutation(first_key, instances)
    tau_order = jax.random.permutation(second_key, instances)
    offsets = jax.random.permutation(third_key, instances)[:ADAPTERS_START]
    sender = jnp.arange(ADAPTER_COUNT) // ADAPTERS_START
    within = jnp.arange(ADAPTER_COUNT) % ADAPTERS_START
    return sigma_order[(tau_order[sender] + offsets[within]) % instances].astype(jnp.int32)


def block_levels(rng, extent, cuts, least, largest):
    def one(dim, blocks):
        heights = jax.random.uniform(jax.random.fold_in(jax.random.fold_in(rng, 6), dim), (blocks,), jnp.float32, least / len(cuts), largest / len(cuts))
        return jnp.repeat(jnp.exp(heights), extent[dim] // blocks).reshape((-1,) + (1,) * (len(extent) - dim - 1))

    level = one(*cuts[0])
    for cut in cuts[1:]:
        level = level * one(*cut)
    return level


def shared_out(own_key, own, number, rows, number_of, top, most, skew):
    order = jax.random.permutation(own_key, number_of)
    packed, common = portions_of(number_of, rows * top, most, skew, True), portions_of(number_of, rows * top, most, skew, False)
    places = jnp.arange(number_of)

    def named(sizes, turn):
        used = int((sizes > 0).sum())
        fixed = max(1, used // 4)
        passed = fixed + (places - fixed + turn * (used - fixed)) % max(1, number_of - fixed)
        return jnp.zeros((number_of,), jnp.int32).at[order[jnp.where(places < fixed, places, passed)]].set(jnp.asarray(sizes, jnp.int32))

    sizes = jnp.where(number % 4 == 0, named(packed, number // 4), named(common, number - number // 4 - 1))
    mixed = jax.random.permutation(jax.random.fold_in(own, 3), number_of)
    donor, taker = mixed[0:number_of // 2 * 2:2], mixed[1:number_of // 2 * 2:2]
    room = jnp.minimum(sizes[donor] - 1, most - sizes[taker]) // 2
    room = jnp.where((donor == order[0]) | (taker == order[0]) | (sizes[taker] == 0), 0, jnp.maximum(room, 0))
    passed = jax.random.randint(jax.random.fold_in(own, 4), (number_of // 2,), 0, 1 << 20) % (room + 1)
    sizes = sizes.at[donor].add(-passed).at[taker].add(passed)
    items = jnp.searchsorted(jnp.cumsum(sizes), jnp.arange(rows * top), side="right").astype(jnp.int32)
    table = items.reshape(top, rows).T
    table = table[jax.random.permutation(jax.random.fold_in(own, 1), rows)]
    turn = jax.random.randint(jax.random.fold_in(own, 2), (rows, 1), 0, top)
    return jnp.take_along_axis(table, (jnp.arange(top)[None, :] + turn) % top, axis=1)


def portions_of(amount, total, bound, slope, full):
    loads = [(1 << 20) // math.isqrt(standing ** slope) + 1 for standing in range(1, amount + 1)]
    largest = bound if full else min(bound, max(-(-total // amount), total * loads[0] // sum(loads)))
    least = 1 if total - largest >= amount - 1 else 0
    counts, surplus = [largest] + [least] * (amount - 1), total - largest - least * (amount - 1)
    while surplus > 0:
        candidates = [i for i in range(1, amount) if counts[i] < largest] or [i for i in range(1, amount) if counts[i] < bound]
        whole, remaining = sum([loads[i] for i in candidates]), surplus
        for i in candidates:
            more = min(bound - counts[i], max(1, remaining * loads[i] // whole), surplus)
            counts[i] = counts[i] + more
            surplus = surplus - more
    return np.array(counts)


def gaussian(own_key, extent, deviation, bound, cuts=(), dtype=jnp.bfloat16):
    values = deviation * jax.random.normal(own_key, extent, jnp.float32)
    if cuts:
        values = values * block_levels(own_key, extent, cuts, -0.22, 0.18)
    return jnp.clip(values, -bound, bound).astype(dtype)


def setup_inputs(seed: int = 0, part: int = 0) -> dict:
    splits = jax.random.split(jax.random.key(seed), 11)
    own_keys = jax.random.split(jax.random.fold_in(splits[10], part), 11)
    tokens = gaussian(own_keys[0], (DECODE_STEPS, REQUEST_ROWS, FEATURES_IN), 1.0, 6.0, ((1, 8), (2, 2)))
    queries = draw_queries(jax.random.fold_in(jax.random.fold_in(splits[10], part), 71), part)
    key_value_cache = draw_key_value_cache(jax.random.fold_in(jax.random.fold_in(splits[10], part), 71), part)
    key_value_length = draw_key_value_length(jax.random.fold_in(jax.random.fold_in(splits[10], part), 71), part)
    request_adapter_index_keys = jax.random.split(jax.random.fold_in(own_keys[4], 1), REQUEST_ROWS // R_INST)
    request_adapter_index_turns = jax.random.permutation(jax.random.fold_in(own_keys[4], 3), REQUEST_ROWS // R_INST)
    request_adapter_index = jax.vmap(lambda own, number: shared_out(jax.random.fold_in(own_keys[4], 2), own, number, R_INST, ADAPTERS_START, 1, SEG, 2))(request_adapter_index_keys, request_adapter_index_turns).reshape((REQUEST_ROWS, 1))
    adapter_destination = draw_adapter_destination(jax.random.fold_in(jax.random.fold_in(splits[10], part), 71), part)
    key_matrix = gaussian(splits[6], (FEATURES_IN, KEY_VALUE_WIDTH), FEATURES_IN ** -0.5, 0.09375, ((0, 2),))
    value_matrix = gaussian(splits[7], (FEATURES_IN, KEY_VALUE_WIDTH), FEATURES_IN ** -0.5, 0.09375, ((0, 2),))
    adapter_down_maps = gaussian(own_keys[8], (ADAPTER_COUNT, FEATURES_IN, 2 * ADAPTER_RANK), FEATURES_IN ** -0.5, 0.09375, ((0, 8), (1, 2)))
    adapter_up_maps = gaussian(own_keys[9], (ADAPTER_COUNT, 2, ADAPTER_RANK, KEY_VALUE_WIDTH), ADAPTER_RANK ** -0.5, 0.75, ((0, 8), (3, 2)))
    return dict(tokens=tokens, queries=queries, key_value_cache=key_value_cache, key_value_length=key_value_length, request_adapter_index=request_adapter_index, adapter_destination=adapter_destination, key_matrix=key_matrix, value_matrix=value_matrix, adapter_down_maps=adapter_down_maps, adapter_up_maps=adapter_up_maps)


def reference(tokens, queries, key_value_cache, key_value_length, request_adapter_index, adapter_destination, key_matrix, value_matrix, adapter_down_maps, adapter_up_maps):
    chosen_adapter = request_adapter_index[:, 0].astype(jnp.int32)
    home_of = (jnp.arange(REQUEST_ROWS) // R_INST).astype(jnp.int32)
    adapter_of = home_of * ADAPTERS_START + chosen_adapter
    flat_tokens = tokens.reshape(DECODE_STEPS * REQUEST_ROWS, FEATURES_IN)
    base_key = jnp.dot(flat_tokens, key_matrix, preferred_element_type=jnp.float32)
    base_value = jnp.dot(flat_tokens, value_matrix, preferred_element_type=jnp.float32)
    base_both = jnp.stack([base_key, base_value], axis=1).reshape(DECODE_STEPS, REQUEST_ROWS, 2, KEY_VALUE_WIDTH)
    grouped = tokens.reshape(DECODE_STEPS, N_INST, R_INST, FEATURES_IN).astype(jnp.float32)
    down_map_blocks = adapter_down_maps.reshape(N_INST, ADAPTERS_START, FEATURES_IN, 2 * ADAPTER_RANK).astype(jnp.float32)
    low_every = jnp.einsum("tird,isdk->tirsk", grouped, down_map_blocks)
    low_every = lax.optimization_barrier(low_every.astype(jnp.bfloat16)).astype(jnp.float32)
    member = (chosen_adapter.reshape(N_INST, R_INST)[:, :, None] == jnp.arange(ADAPTERS_START)[None, None, :]).astype(jnp.float32)
    low_pick = (low_every * member[None, :, :, :, None]).reshape(DECODE_STEPS, N_INST, R_INST, ADAPTERS_START, 2, ADAPTER_RANK)
    up_map_blocks = adapter_up_maps.reshape(N_INST, ADAPTERS_START, 2, ADAPTER_RANK, KEY_VALUE_WIDTH).astype(jnp.float32)
    adapter_term = jnp.einsum("tirsck,iscko->tirco", low_pick, up_map_blocks).reshape(DECODE_STEPS, REQUEST_ROWS, 2, KEY_VALUE_WIDTH)
    fresh_kv = (base_both + adapter_term).astype(jnp.bfloat16)
    fresh_wide_rows = lax.optimization_barrier(fresh_kv).astype(jnp.float32)
    query_head_rows = queries.astype(jnp.float32).reshape(DECODE_STEPS, REQUEST_ROWS, KEY_VALUE_HEADS, QUERY_GROUP, HEAD_SIZE)
    cached_state = key_value_cache.astype(jnp.float32)
    previous_keys = cached_state[:, :, 0].reshape(REQUEST_ROWS, CONTEXT_LENGTH, KEY_VALUE_HEADS, HEAD_SIZE)
    previous_values = cached_state[:, :, 1].reshape(REQUEST_ROWS, CONTEXT_LENGTH, KEY_VALUE_HEADS, HEAD_SIZE)
    appended_keys = fresh_wide_rows[:, :, 0].reshape(DECODE_STEPS, REQUEST_ROWS, KEY_VALUE_HEADS, HEAD_SIZE)
    appended_values = fresh_wide_rows[:, :, 1].reshape(DECODE_STEPS, REQUEST_ROWS, KEY_VALUE_HEADS, HEAD_SIZE)
    factor = HEAD_SIZE ** -0.5
    old_scores = jnp.einsum("trghd,rpgd->trghp", query_head_rows, previous_keys) * factor
    visible = jnp.arange(CONTEXT_LENGTH).astype(jnp.int32)[None, :] < key_value_length[:, None]
    old_scores = jnp.where(visible[None, :, None, None, :], old_scores, -jnp.inf)
    new_scores = jnp.einsum("trghd,urgd->trghu", query_head_rows, appended_keys) * factor
    causal = jnp.arange(DECODE_STEPS)[None, :] <= jnp.arange(DECODE_STEPS)[:, None]
    new_scores = jnp.where(causal[:, None, None, None, :], new_scores, -jnp.inf)
    scores = jnp.concatenate([old_scores, new_scores], axis=-1)
    highest = jnp.max(scores, axis=-1, keepdims=True)
    expo = jnp.exp(scores - highest)
    weights = expo / jnp.sum(expo, axis=-1, keepdims=True)
    weights = lax.optimization_barrier(weights.astype(jnp.bfloat16)).astype(jnp.float32)
    served = jnp.einsum("trghp,rpgd->trghd", weights[..., :CONTEXT_LENGTH], previous_values)
    served = served + jnp.einsum("trghu,urgd->trghd", weights[..., CONTEXT_LENGTH:], appended_values)
    served = served.reshape(DECODE_STEPS, REQUEST_ROWS, HQW).astype(jnp.bfloat16)
    destination = adapter_destination[adapter_of].astype(jnp.int32)
    plan_hits = (adapter_destination[:, None] == jnp.arange(N_INST).astype(jnp.int32)[None, :]).astype(jnp.int32)
    earlier = jnp.cumsum(plan_hits, axis=0) - plan_hits
    slot_rank = jnp.sum(earlier * plan_hits, axis=1).astype(jnp.int32)
    row_hits = (chosen_adapter.reshape(N_INST, R_INST)[:, :, None] == jnp.arange(ADAPTERS_START).astype(jnp.int32)[None, None, :]).astype(jnp.int32)
    position = jnp.sum((jnp.cumsum(row_hits, axis=1) - row_hits) * row_hits, axis=2).reshape(REQUEST_ROWS)
    target = ((destination * ADAPTERS_START + slot_rank[adapter_of]) * SEG + position).astype(jnp.int32)
    attended = jnp.zeros((DECODE_STEPS, DROWS, HQW), jnp.bfloat16).at[:, target].set(served)
    new_kv = jnp.zeros((DECODE_STEPS, DROWS, 2, KEY_VALUE_WIDTH), jnp.bfloat16).at[:, target].set(fresh_kv)
    return attended, new_kv
```

```python
import functools

import jax
import jax.numpy as jnp
from jax import lax
from jax.experimental import pallas as pl
from jax.experimental.pallas import tpu as pltpu
from jax.sharding import PartitionSpec as P

QUERY_GROUP = 8
HEAD_SIZE = 128
SEG = 24
NB = 16
LANE = 16
VMEM_LIMIT = 48 * 1024 * 1024


def project_kernel(
    part_ref, tok_ref, key_ref, value_ref, down_ref, idx_ref,
    other_key, other_value, mine_key, mine_value, low_ref,
):
    j = pl.program_id(0)
    half = pl.num_programs(0) // 2
    tok = tok_ref[...]
    key_part = jnp.dot(tok, key_ref[...], preferred_element_type=jnp.float32)
    value_part = jnp.dot(tok, value_ref[...], preferred_element_type=jnp.float32)

    @pl.when(j < half)
    def _():
        other_key[...] = key_part
        other_value[...] = value_part

    @pl.when(j >= half)
    def _():
        mine_key[...] = key_part
        mine_value[...] = value_part

    each = down_ref.shape[0]
    total = jnp.where(j == 0, 0.0, low_ref[...])
    for a in range(each):
        low = jnp.dot(tok, down_ref[a], preferred_element_type=jnp.float32)
        total = jnp.where(idx_ref[...] == j * each + a, low, total)
    low_ref[...] = total


def project(tokens, key_matrix, value_matrix, down, idx):
    rows, depth = tokens.shape
    slots, _, rank = down.shape
    width = key_matrix.shape[1]
    steps = 4
    tile = width // steps
    per = slots // steps
    half = steps // 2
    part = lax.axis_index("tp").astype(jnp.int32).reshape(1)

    def columns(j, part_ref):
        return (0, lax.rem((1 - part_ref[0]) * half + j, steps))

    other = pl.BlockSpec((rows, tile), lambda j, p: (0, jnp.minimum(j, half - 1)))
    mine = pl.BlockSpec((rows, tile), lambda j, p: (0, jnp.maximum(j - half, 0)))
    out = jax.ShapeDtypeStruct((rows, width // 2), jnp.float32)
    return pl.pallas_call(
        project_kernel,
        grid_spec=pltpu.PrefetchScalarGridSpec(
            num_scalar_prefetch=1,
            grid=(steps,),
            in_specs=[
                pl.BlockSpec((rows, depth), lambda j, p: (0, 0)),
                pl.BlockSpec((depth, tile), columns),
                pl.BlockSpec((depth, tile), columns),
                pl.BlockSpec((per, depth, rank), lambda j, p: (j, 0, 0)),
                pl.BlockSpec((rows, 1), lambda j, p: (0, 0)),
            ],
            out_specs=[other, other, mine, mine, pl.BlockSpec((rows, rank), lambda j, p: (0, 0))],
        ),
        out_shape=[out, out, out, out, jax.ShapeDtypeStruct((rows, rank), jnp.float32)],
        compiler_params=pltpu.CompilerParams(vmem_limit_bytes=VMEM_LIMIT),
        cost_estimate=pl.CostEstimate(
            flops=2 * rows * depth * (2 * width + slots * rank),
            bytes_accessed=2 * depth * (rows + 2 * width + slots * rank) + 8 * rows * width,
            transcendentals=0,
        ),
        name="project",
    )(part, tokens, key_matrix, value_matrix, down, idx)


def fold_matrix(rows, n_of, p_base, lane_base):
    r = lax.broadcasted_iota(jnp.int32, (rows, 128), 0)
    c = lax.broadcasted_iota(jnp.int32, (rows, 128), 1)
    return (c == lane_base + p_base + r // n_of).astype(jnp.bfloat16)


def weights_kernel(
    steps_t, requests,
    q_ref, k_ref, valid_ref, mk_ref, mv_ref, rk_ref, rv_ref, ml_ref, rl_ref, idx_ref, up_ref,
    fresh_ref, wts_ref,
):
    b = pl.program_id(0)
    width = mk_ref.shape[1]
    heads = width // HEAD_SIZE
    context = k_ref.shape[1] // width

    @pl.when(b == 0)
    def _():
        low = (ml_ref[...] + rl_ref[...]).astype(jnp.bfloat16)
        rank = low.shape[1] // 2
        idx = idx_ref[...]
        key = mk_ref[...] + rk_ref[...]
        value = mv_ref[...] + rv_ref[...]
        for s in range(up_ref.shape[0]):
            part = jnp.where(idx == s, low, jnp.zeros_like(low))
            key += jnp.dot(part[:, :rank], up_ref[s, 0], preferred_element_type=jnp.float32)
            value += jnp.dot(part[:, rank:], up_ref[s, 1], preferred_element_type=jnp.float32)
        fresh_ref[:, :width] = key.astype(jnp.bfloat16)
        fresh_ref[:, width:] = value.astype(jnp.bfloat16)

    rows = QUERY_GROUP * steps_t * NB
    old_lanes = context * NB
    new_lanes = steps_t * NB
    row = lax.broadcasted_iota(jnp.int32, (rows, old_lanes), 0)
    lane = lax.broadcasted_iota(jnp.int32, (rows, old_lanes), 1)
    old_ok = (row % NB == lane % NB) & (valid_ref[0] > 0)
    row = lax.broadcasted_iota(jnp.int32, (rows, new_lanes), 0)
    lane = lax.broadcasted_iota(jnp.int32, (rows, new_lanes), 1)
    new_ok = (row % NB == lane % NB) & (lane // NB <= (row // NB) % steps_t)
    factor = HEAD_SIZE ** (-0.5)
    q = q_ref[...].reshape(steps_t * NB, q_ref.shape[-1])
    k = k_ref[...]
    new_k = [fresh_ref[pl.ds(t * requests + b * NB, NB), :width] for t in range(steps_t)]
    new_k = jnp.concatenate(new_k, axis=0)
    half = rows // 2
    total = jnp.zeros((half, 128), jnp.float32)
    dims = (((1,), (1,)), ((), ()))
    for g in range(heads):
        here = slice(g * HEAD_SIZE, (g + 1) * HEAD_SIZE)
        start = g * QUERY_GROUP * HEAD_SIZE
        qg = jnp.concatenate(
            [q[:, start + h * HEAD_SIZE : start + (h + 1) * HEAD_SIZE] for h in range(QUERY_GROUP)],
            axis=0,
        )
        kg = jnp.concatenate(
            [k[:, p * width + g * HEAD_SIZE : p * width + (g + 1) * HEAD_SIZE] for p in range(context)],
            axis=0,
        )
        old = lax.dot_general(qg, kg, dims, preferred_element_type=jnp.float32) * factor
        new = lax.dot_general(qg, new_k[:, here], dims, preferred_element_type=jnp.float32) * factor
        old = jnp.where(old_ok, old, -jnp.inf)
        new = jnp.where(new_ok, new, -jnp.inf)
        top = jnp.maximum(
            jnp.max(old, axis=1, keepdims=True), jnp.max(new, axis=1, keepdims=True)
        )
        old = jnp.exp(old - top)
        new = jnp.exp(new - top)
        norm = jnp.sum(old, axis=1, keepdims=True) + jnp.sum(new, axis=1, keepdims=True)
        scale = 1.0 / norm
        old = (old * scale).astype(jnp.bfloat16)
        new = (new * scale).astype(jnp.bfloat16)
        for part in range(2):
            base = part * 64 + g * LANE
            span = slice(part * half, (part + 1) * half)
            total += jnp.dot(
                old[span], fold_matrix(old_lanes, NB, 0, base), preferred_element_type=jnp.float32
            )
            total += jnp.dot(
                new[span], fold_matrix(new_lanes, NB, context, base),
                preferred_element_type=jnp.float32,
            )
    total = total.astype(jnp.bfloat16)
    for i in range(half // NB):
        wts_ref[:, i * 128 : (i + 1) * 128] = total[i * NB : (i + 1) * NB]


def weigh(queries, keys, valid, mine, received, low_mine, low_received, idx, up):
    steps_t, requests, query_width = queries.shape
    rows, width = mine[0].shape
    blocks = requests // NB
    context = keys.shape[1] // width
    whole = lambda a: pl.BlockSpec(a.shape, lambda b: (0,) * a.ndim)
    packed = QUERY_GROUP * steps_t // 2 * 128
    return pl.pallas_call(
        functools.partial(weights_kernel, steps_t, requests),
        grid=(blocks,),
        in_specs=[
            pl.BlockSpec((steps_t, NB, query_width), lambda b: (0, b, 0)),
            pl.BlockSpec((NB, keys.shape[1]), lambda b: (b, 0)),
            pl.BlockSpec((1, 1, context * NB), lambda b: (b, 0, 0)),
        ]
        + [whole(a) for a in (*mine, *received, low_mine, low_received, idx, up)],
        out_specs=[
            pl.BlockSpec((rows, 2 * width), lambda b: (0, 0)),
            pl.BlockSpec((NB, packed), lambda b: (b, 0)),
        ],
        out_shape=[
            jax.ShapeDtypeStruct((rows, 2 * width), jnp.bfloat16),
            jax.ShapeDtypeStruct((requests, packed), jnp.bfloat16),
        ],
        compiler_params=pltpu.CompilerParams(vmem_limit_bytes=VMEM_LIMIT),
        cost_estimate=pl.CostEstimate(
            flops=10 ** 10, bytes_accessed=2 * 10 ** 7, transcendentals=10 ** 6
        ),
        name="weigh",
    )(queries, keys, valid, *mine, *received, low_mine, low_received, idx, up)


def serve_kernel(steps_t, width, v_ref, f_ref, w_ref, out_ref):
    heads = width // HEAD_SIZE
    context = v_ref.shape[1] // width
    rows = QUERY_GROUP * steps_t * NB
    half = rows // 2
    lanes = (context + steps_t) * NB
    row = lax.broadcasted_iota(jnp.int32, (rows, lanes), 0)
    lane = lax.broadcasted_iota(jnp.int32, (rows, lanes), 1)
    own = row % NB == lane % NB
    w = w_ref[...]
    w = jnp.concatenate([w[:, i * 128 : (i + 1) * 128] for i in range(half // NB)], axis=0)
    r = lax.broadcasted_iota(jnp.int32, (128, lanes), 0)
    c = lax.broadcasted_iota(jnp.int32, (128, lanes), 1)
    v = v_ref[...]
    fresh = f_ref[...]
    for g in range(heads):
        vg = [v[:, p * width + g * HEAD_SIZE : p * width + (g + 1) * HEAD_SIZE] for p in range(context)]
        for t in range(steps_t):
            start = (2 * t + 1) * width + g * HEAD_SIZE
            vg.append(fresh[:, start : start + HEAD_SIZE])
        vg = jnp.concatenate(vg, axis=0)
        wide = []
        for part in range(2):
            spread = (r == part * 64 + g * LANE + c // NB).astype(jnp.bfloat16)
            wide.append(jnp.dot(w, spread, preferred_element_type=jnp.float32))
        wide = jnp.concatenate(wide, axis=0)
        wide = jnp.where(own, wide, 0.0).astype(jnp.bfloat16)
        res = jnp.dot(wide, vg, preferred_element_type=jnp.float32).astype(jnp.bfloat16)
        for h in range(QUERY_GROUP):
            start = (g * QUERY_GROUP + h) * HEAD_SIZE
            out_ref[:, :, start : start + HEAD_SIZE] = res[
                h * steps_t * NB : (h + 1) * steps_t * NB
            ].reshape(steps_t, NB, HEAD_SIZE)


def serve(values, second, steps_t, width):
    rows = values.shape[0]
    query_width = width * QUERY_GROUP
    fresh_width = steps_t * 2 * width
    packed = second.shape[1] - fresh_width
    return pl.pallas_call(
        functools.partial(serve_kernel, steps_t, width),
        grid=(rows // NB,),
        in_specs=[
            pl.BlockSpec((NB, values.shape[1]), lambda b: (b, 0)),
            pl.BlockSpec((NB, fresh_width), lambda b: (b, 0)),
            pl.BlockSpec((NB, packed), lambda b: (b, fresh_width // packed)),
        ],
        out_specs=pl.BlockSpec((steps_t, NB, query_width), lambda b: (0, b, 0)),
        out_shape=jax.ShapeDtypeStruct((steps_t, rows, query_width), jnp.bfloat16),
        compiler_params=pltpu.CompilerParams(vmem_limit_bytes=VMEM_LIMIT),
        cost_estimate=pl.CostEstimate(
            flops=10 ** 10, bytes_accessed=10 ** 7, transcendentals=0
        ),
        name="serve",
    )(values, second, second)


def on_device(
    tokens,
    queries,
    key_value_cache,
    key_value_length,
    request_adapter_index,
    adapter_destination,
    key_matrix,
    value_matrix,
    adapter_down_maps,
    adapter_up_maps,
):
    slot_count = adapter_down_maps.shape[0]
    requests = request_adapter_index.shape[0]
    steps_t = tokens.shape[0]
    context = key_value_cache.shape[1]
    width = key_value_cache.shape[3]
    instances = lax.axis_size("inst")
    own_index = lax.axis_index("inst")
    chosen = request_adapter_index[:, 0]
    order = jnp.arange(requests)
    same = (chosen[:, None] == chosen[None, :]) & (order[:, None] > order[None, :])
    within = jnp.sum(same.astype(jnp.int32), axis=1)
    leaving = lax.dynamic_slice_in_dim(adapter_destination, own_index * slot_count, slot_count)
    towards = jnp.sum(
        jnp.where(chosen[:, None] == jnp.arange(slot_count)[None, :], leaving[None, :], 0), axis=1
    )
    seat = towards * SEG + within
    pick = (seat[None, :] == jnp.arange(instances * SEG)[:, None]).astype(jnp.bfloat16)

    def move(rows):
        sent = jnp.dot(pick, rows, preferred_element_type=jnp.float32).astype(jnp.bfloat16)
        sent = sent.reshape(instances, SEG, rows.shape[1])
        got = lax.all_to_all(sent, "inst", split_axis=0, concat_axis=0, tiled=True)
        if instances != slot_count:
            coming = jnp.sum(
                (adapter_destination.reshape(instances, slot_count) == own_index).astype(jnp.int32),
                axis=1,
            )
            rank = jnp.cumsum(coming) - 1
            hit = coming[None, :] * (rank[None, :] == jnp.arange(slot_count)[:, None])
            anchor = jnp.sum(hit * jnp.arange(instances)[None, :], axis=1)
            got = jnp.take(got, anchor, axis=0)
        return got.reshape(slot_count * SEG, rows.shape[1])

    values = move(key_value_cache[:, :, 1].reshape(requests, context * width))
    keys = key_value_cache[:, :, 0].reshape(requests, context * width)
    idx = jnp.tile(chosen, steps_t)[:, None]
    other_key, other_value, mine_key, mine_value, low = project(
        tokens.reshape(steps_t * requests, -1), key_matrix, value_matrix, adapter_down_maps, idx
    )
    swap = lambda a: lax.ppermute(a, "tp", [(0, 1), (1, 0)])
    valid = (jnp.arange(context)[None, :, None] < key_value_length.reshape(-1, 1, NB)).astype(
        jnp.int32
    )
    fresh, weights = weigh(
        queries,
        keys,
        valid.reshape(-1, 1, context * NB),
        (mine_key, mine_value),
        (swap(other_key), swap(other_value)),
        low,
        swap(low),
        idx,
        adapter_up_maps,
    )
    second = jnp.concatenate([fresh[t * requests : (t + 1) * requests] for t in range(steps_t)] + [weights], axis=1)
    second = move(second)
    attended = serve(values, second, steps_t, width)
    new_kv = second[:, : steps_t * 2 * width].reshape(-1, steps_t, 2, width)
    return (attended, jnp.swapaxes(new_kv, 0, 1))


def solution(mesh):
    return jax.shard_map(
        on_device,
        mesh=mesh,
        in_specs=(
            P(None, ("grp", "inst"), "tp"),
            P(None, ("grp", "inst"), "tp"),
            P(("grp", "inst"), None, None, "tp"),
            P(("grp", "inst")),
            P(("grp", "inst"), None),
            P("grp"),
            P("tp", None),
            P("tp", None),
            P(("grp", "inst"), "tp", None),
            P(("grp", "inst"), None, None, "tp"),
        ),
        out_specs=(P(None, ("grp", "inst"), "tp"), P(None, ("grp", "inst"), None, "tp")),
        check_vma=False,
    )
```

```python
import functools

import jax
import jax.numpy as jnp
from jax import lax
from jax.experimental import pallas as pl
from jax.experimental.pallas import tpu as pltpu
from jax.sharding import PartitionSpec as P

QUERY_GROUP = 8
HEAD_SIZE = 128
SEG = 24
NB = 16
LANE = 16
VMEM_LIMIT = 48 * 1024 * 1024


def project_kernel(
    part_ref, tok_ref, key_ref, value_ref, down_ref, idx_ref,
    other_key, other_value, mine_key, mine_value, low_ref,
):
    j = pl.program_id(0)
    half = pl.num_programs(0) // 2
    tok = tok_ref[...]
    key_part = jnp.dot(tok, key_ref[...], preferred_element_type=jnp.float32)
    value_part = jnp.dot(tok, value_ref[...], preferred_element_type=jnp.float32)

    @pl.when(j < half)
    def _():
        other_key[...] = key_part
        other_value[...] = value_part

    @pl.when(j >= half)
    def _():
        mine_key[...] = key_part
        mine_value[...] = value_part

    each = down_ref.shape[0]
    total = jnp.where(j == 0, 0.0, low_ref[...])
    for a in range(each):
        low = jnp.dot(tok, down_ref[a], preferred_element_type=jnp.float32)
        total = jnp.where(idx_ref[...] == j * each + a, low, total)
    low_ref[...] = total


def project(tokens, key_matrix, value_matrix, down, idx):
    rows, depth = tokens.shape
    slots, _, rank = down.shape
    width = key_matrix.shape[1]
    steps = 4
    tile = width // steps
    per = slots // steps
    half = steps // 2
    part = lax.axis_index("tp").astype(jnp.int32).reshape(1)

    def columns(j, part_ref):
        return (0, lax.rem((1 - part_ref[0]) * half + j, steps))

    other = pl.BlockSpec((rows, tile), lambda j, p: (0, jnp.minimum(j, half - 1)))
    mine = pl.BlockSpec((rows, tile), lambda j, p: (0, jnp.maximum(j - half, 0)))
    out = jax.ShapeDtypeStruct((rows, width // 2), jnp.float32)
    return pl.pallas_call(
        project_kernel,
        grid_spec=pltpu.PrefetchScalarGridSpec(
            num_scalar_prefetch=1,
            grid=(steps,),
            in_specs=[
                pl.BlockSpec((rows, depth), lambda j, p: (0, 0)),
                pl.BlockSpec((depth, tile), columns),
                pl.BlockSpec((depth, tile), columns),
                pl.BlockSpec((per, depth, rank), lambda j, p: (j, 0, 0)),
                pl.BlockSpec((rows, 1), lambda j, p: (0, 0)),
            ],
            out_specs=[other, other, mine, mine, pl.BlockSpec((rows, rank), lambda j, p: (0, 0))],
        ),
        out_shape=[out, out, out, out, jax.ShapeDtypeStruct((rows, rank), jnp.float32)],
        compiler_params=pltpu.CompilerParams(vmem_limit_bytes=VMEM_LIMIT),
        cost_estimate=pl.CostEstimate(
            flops=2 * rows * depth * (2 * width + slots * rank),
            bytes_accessed=2 * depth * (rows + 2 * width + slots * rank) + 8 * rows * width,
            transcendentals=0,
        ),
        name="project",
    )(part, tokens, key_matrix, value_matrix, down, idx)


def split_kernel(leaving_ref, row_ref, col_ref, cache_ref, sent_ref, keys_ref, pick_ref, vals):
    requests = col_ref.shape[0]
    width = cache_ref.shape[1]
    context = keys_ref.shape[1] // width
    block = 2 * context * NB
    chosen = row_ref[...]
    r = lax.broadcasted_iota(jnp.int32, (requests, requests), 0)
    c = lax.broadcasted_iota(jnp.int32, (requests, requests), 1)
    same = jnp.where((col_ref[...] == chosen) & (r < c), 1, 0)
    seat = jnp.sum(same, axis=0, keepdims=True)
    for a in range(leaving_ref.shape[0]):
        seat += jnp.where(chosen == a, leaving_ref[a] * SEG, 0)
    slots = pick_ref.shape[0]
    pick = lax.broadcasted_iota(jnp.int32, (slots, requests), 0) == seat
    pick = pick.astype(jnp.bfloat16)
    pick_ref[...] = pick
    r = lax.broadcasted_iota(jnp.int32, (block // 2, block), 0)
    c = lax.broadcasted_iota(jnp.int32, (block // 2, block), 1)
    first = (r % NB) * (2 * context) + (r // NB) * 2
    take_key = (c == first).astype(jnp.bfloat16)
    take_value = (c == first + 1).astype(jnp.bfloat16)
    for b in range(requests // NB):
        x = cache_ref[b * block : (b + 1) * block]
        k = jnp.dot(take_key, x, preferred_element_type=jnp.float32).astype(jnp.bfloat16)
        v = jnp.dot(take_value, x, preferred_element_type=jnp.float32).astype(jnp.bfloat16)
        here = slice(b * NB, (b + 1) * NB)
        for p in range(context):
            lanes = slice(p * width, (p + 1) * width)
            keys_ref[here, lanes] = k[p * NB : (p + 1) * NB]
            vals[here, lanes] = v[p * NB : (p + 1) * NB]
    for p in range(context):
        lanes = slice(p * width, (p + 1) * width)
        moved = jnp.dot(pick, vals[:, lanes], preferred_element_type=jnp.float32)
        sent_ref[:, lanes] = moved.astype(jnp.bfloat16)


def split(cache, chosen, leaving, slots):
    requests, context, _, width = cache.shape
    vmem = pl.BlockSpec(memory_space=pltpu.VMEM)
    wide = context * width
    return pl.pallas_call(
        split_kernel,
        in_specs=[pl.BlockSpec(memory_space=pltpu.SMEM), vmem, vmem, vmem],
        out_specs=[vmem, vmem, vmem],
        out_shape=[
            jax.ShapeDtypeStruct((slots, wide), jnp.bfloat16),
            jax.ShapeDtypeStruct((requests, wide), jnp.bfloat16),
            jax.ShapeDtypeStruct((slots, requests), jnp.bfloat16),
        ],
        scratch_shapes=[pltpu.VMEM((requests, wide), jnp.bfloat16)],
        compiler_params=pltpu.CompilerParams(vmem_limit_bytes=VMEM_LIMIT),
        cost_estimate=pl.CostEstimate(
            flops=10 ** 9, bytes_accessed=2 * (slots + 3 * requests) * wide, transcendentals=0
        ),
        name="split",
    )(leaving, chosen[None, :], chosen[:, None], cache.reshape(-1, width))


def fold_matrix(rows, n_of, p_base, lane_base):
    r = lax.broadcasted_iota(jnp.int32, (rows, 128), 0)
    c = lax.broadcasted_iota(jnp.int32, (rows, 128), 1)
    return (c == lane_base + p_base + r // n_of).astype(jnp.bfloat16)


def weights_kernel(
    steps_t, requests,
    q_ref, k_ref, valid_ref, mk_ref, mv_ref, rk_ref, rv_ref, ml_ref, rl_ref, idx_ref, up_ref,
    fresh_ref, wts_ref,
):
    b = pl.program_id(0)
    width = mk_ref.shape[1]
    heads = width // HEAD_SIZE
    context = k_ref.shape[1] // width

    @pl.when(b == 0)
    def _():
        low = (ml_ref[...] + rl_ref[...]).astype(jnp.bfloat16)
        rank = low.shape[1] // 2
        idx = idx_ref[...]
        key = mk_ref[...] + rk_ref[...]
        value = mv_ref[...] + rv_ref[...]
        for s in range(up_ref.shape[0]):
            part = jnp.where(idx == s, low, jnp.zeros_like(low))
            key += jnp.dot(part[:, :rank], up_ref[s, 0], preferred_element_type=jnp.float32)
            value += jnp.dot(part[:, rank:], up_ref[s, 1], preferred_element_type=jnp.float32)
        fresh_ref[:, :width] = key.astype(jnp.bfloat16)
        fresh_ref[:, width:] = value.astype(jnp.bfloat16)

    rows = QUERY_GROUP * steps_t * NB
    old_lanes = context * NB
    new_lanes = steps_t * NB
    row = lax.broadcasted_iota(jnp.int32, (rows, old_lanes), 0)
    lane = lax.broadcasted_iota(jnp.int32, (rows, old_lanes), 1)
    old_ok = (row % NB == lane % NB) & (valid_ref[0] > 0)
    row = lax.broadcasted_iota(jnp.int32, (rows, new_lanes), 0)
    lane = lax.broadcasted_iota(jnp.int32, (rows, new_lanes), 1)
    new_ok = (row % NB == lane % NB) & (lane // NB <= (row // NB) % steps_t)
    factor = HEAD_SIZE ** (-0.5)
    q = q_ref[...].reshape(steps_t * NB, q_ref.shape[-1])
    k = k_ref[...]
    new_k = [fresh_ref[pl.ds(t * requests + b * NB, NB), :width] for t in range(steps_t)]
    new_k = jnp.concatenate(new_k, axis=0)
    half = rows // 2
    total = jnp.zeros((half, 128), jnp.float32)
    dims = (((1,), (1,)), ((), ()))
    for g in range(heads):
        here = slice(g * HEAD_SIZE, (g + 1) * HEAD_SIZE)
        start = g * QUERY_GROUP * HEAD_SIZE
        qg = jnp.concatenate(
            [q[:, start + h * HEAD_SIZE : start + (h + 1) * HEAD_SIZE] for h in range(QUERY_GROUP)],
            axis=0,
        )
        kg = jnp.concatenate(
            [k[:, p * width + g * HEAD_SIZE : p * width + (g + 1) * HEAD_SIZE] for p in range(context)],
            axis=0,
        )
        old = lax.dot_general(qg, kg, dims, preferred_element_type=jnp.float32) * factor
        new = lax.dot_general(qg, new_k[:, here], dims, preferred_element_type=jnp.float32) * factor
        old = jnp.where(old_ok, old, -jnp.inf)
        new = jnp.where(new_ok, new, -jnp.inf)
        top = jnp.maximum(
            jnp.max(old, axis=1, keepdims=True), jnp.max(new, axis=1, keepdims=True)
        )
        old = jnp.exp(old - top)
        new = jnp.exp(new - top)
        norm = jnp.sum(old, axis=1, keepdims=True) + jnp.sum(new, axis=1, keepdims=True)
        scale = 1.0 / norm
        old = (old * scale).astype(jnp.bfloat16)
        new = (new * scale).astype(jnp.bfloat16)
        for part in range(2):
            base = part * 64 + g * LANE
            span = slice(part * half, (part + 1) * half)
            total += jnp.dot(
                old[span], fold_matrix(old_lanes, NB, 0, base), preferred_element_type=jnp.float32
            )
            total += jnp.dot(
                new[span], fold_matrix(new_lanes, NB, context, base),
                preferred_element_type=jnp.float32,
            )
    total = total.astype(jnp.bfloat16)
    for i in range(half // NB):
        wts_ref[:, i * 128 : (i + 1) * 128] = total[i * NB : (i + 1) * NB]


def weigh(queries, keys, valid, mine, received, low_mine, low_received, idx, up):
    steps_t, requests, query_width = queries.shape
    rows, width = mine[0].shape
    blocks = requests // NB
    context = keys.shape[1] // width
    whole = lambda a: pl.BlockSpec(a.shape, lambda b: (0,) * a.ndim)
    packed = QUERY_GROUP * steps_t // 2 * 128
    return pl.pallas_call(
        functools.partial(weights_kernel, steps_t, requests),
        grid=(blocks,),
        in_specs=[
            pl.BlockSpec((steps_t, NB, query_width), lambda b: (0, b, 0)),
            pl.BlockSpec((NB, keys.shape[1]), lambda b: (b, 0)),
            pl.BlockSpec((1, 1, context * NB), lambda b: (b, 0, 0)),
        ]
        + [whole(a) for a in (*mine, *received, low_mine, low_received, idx, up)],
        out_specs=[
            pl.BlockSpec((rows, 2 * width), lambda b: (0, 0)),
            pl.BlockSpec((NB, packed), lambda b: (b, 0)),
        ],
        out_shape=[
            jax.ShapeDtypeStruct((rows, 2 * width), jnp.bfloat16),
            jax.ShapeDtypeStruct((requests, packed), jnp.bfloat16),
        ],
        compiler_params=pltpu.CompilerParams(vmem_limit_bytes=VMEM_LIMIT),
        cost_estimate=pl.CostEstimate(
            flops=10 ** 10, bytes_accessed=2 * 10 ** 7, transcendentals=10 ** 6
        ),
        name="weigh",
    )(queries, keys, valid, *mine, *received, low_mine, low_received, idx, up)


def serve_kernel(steps_t, width, v_ref, f_ref, w_ref, out_ref, kv_ref):
    heads = width // HEAD_SIZE
    context = v_ref.shape[1] // width
    rows = QUERY_GROUP * steps_t * NB
    half = rows // 2
    lanes = (context + steps_t) * NB
    row = lax.broadcasted_iota(jnp.int32, (rows, lanes), 0)
    lane = lax.broadcasted_iota(jnp.int32, (rows, lanes), 1)
    own = row % NB == lane % NB
    w = w_ref[...]
    w = jnp.concatenate([w[:, i * 128 : (i + 1) * 128] for i in range(half // NB)], axis=0)
    r = lax.broadcasted_iota(jnp.int32, (128, lanes), 0)
    c = lax.broadcasted_iota(jnp.int32, (128, lanes), 1)
    v = v_ref[...]
    fresh = f_ref[...]
    r2 = lax.broadcasted_iota(jnp.int32, (2 * NB, 2 * NB), 0)
    c2 = lax.broadcasted_iota(jnp.int32, (2 * NB, 2 * NB), 1)
    weave = (c2 == (r2 % 2) * NB + r2 // 2).astype(jnp.bfloat16)
    for t in range(steps_t):
        pair = [fresh[:, (2 * t + i) * width : (2 * t + i + 1) * width] for i in range(2)]
        pair = jnp.dot(
            weave, jnp.concatenate(pair, axis=0), preferred_element_type=jnp.float32
        )
        kv_ref[t] = pair.reshape(NB, 2, width).astype(jnp.bfloat16)
    for g in range(heads):
        vg = [v[:, p * width + g * HEAD_SIZE : p * width + (g + 1) * HEAD_SIZE] for p in range(context)]
        for t in range(steps_t):
            start = (2 * t + 1) * width + g * HEAD_SIZE
            vg.append(fresh[:, start : start + HEAD_SIZE])
        vg = jnp.concatenate(vg, axis=0)
        wide = []
        for part in range(2):
            spread = (r == part * 64 + g * LANE + c // NB).astype(jnp.bfloat16)
            wide.append(jnp.dot(w, spread, preferred_element_type=jnp.float32))
        wide = jnp.concatenate(wide, axis=0)
        wide = jnp.where(own, wide, 0.0).astype(jnp.bfloat16)
        res = jnp.dot(wide, vg, preferred_element_type=jnp.float32).astype(jnp.bfloat16)
        for h in range(QUERY_GROUP):
            start = (g * QUERY_GROUP + h) * HEAD_SIZE
            out_ref[:, :, start : start + HEAD_SIZE] = res[
                h * steps_t * NB : (h + 1) * steps_t * NB
            ].reshape(steps_t, NB, HEAD_SIZE)


def serve(values, second, steps_t, width):
    rows = values.shape[0]
    query_width = width * QUERY_GROUP
    fresh_width = steps_t * 2 * width
    packed = second.shape[1] - fresh_width
    return pl.pallas_call(
        functools.partial(serve_kernel, steps_t, width),
        grid=(rows // NB,),
        in_specs=[
            pl.BlockSpec((NB, values.shape[1]), lambda b: (b, 0)),
            pl.BlockSpec((NB, fresh_width), lambda b: (b, 0)),
            pl.BlockSpec((NB, packed), lambda b: (b, fresh_width // packed)),
        ],
        out_specs=[
            pl.BlockSpec((steps_t, NB, query_width), lambda b: (0, b, 0)),
            pl.BlockSpec((steps_t, NB, 2, width), lambda b: (0, b, 0, 0)),
        ],
        out_shape=[
            jax.ShapeDtypeStruct((steps_t, rows, query_width), jnp.bfloat16),
            jax.ShapeDtypeStruct((steps_t, rows, 2, width), jnp.bfloat16),
        ],
        compiler_params=pltpu.CompilerParams(vmem_limit_bytes=VMEM_LIMIT),
        cost_estimate=pl.CostEstimate(
            flops=10 ** 10, bytes_accessed=10 ** 7, transcendentals=0
        ),
        name="serve",
    )(values, second, second)


def on_device(
    tokens,
    queries,
    key_value_cache,
    key_value_length,
    request_adapter_index,
    adapter_destination,
    key_matrix,
    value_matrix,
    adapter_down_maps,
    adapter_up_maps,
):
    slot_count = adapter_down_maps.shape[0]
    requests = request_adapter_index.shape[0]
    steps_t = tokens.shape[0]
    context = key_value_cache.shape[1]
    width = key_value_cache.shape[3]
    instances = lax.axis_size("inst")
    own_index = lax.axis_index("inst")
    chosen = request_adapter_index[:, 0]
    leaving = lax.dynamic_slice_in_dim(adapter_destination, own_index * slot_count, slot_count)
    sent, keys, pick = split(key_value_cache, chosen, leaving, instances * SEG)

    def move(sent):
        sent = sent.reshape(instances, SEG, sent.shape[1])
        got = lax.all_to_all(sent, "inst", split_axis=0, concat_axis=0, tiled=True)
        if instances != slot_count:
            coming = jnp.sum(
                (adapter_destination.reshape(instances, slot_count) == own_index).astype(jnp.int32),
                axis=1,
            )
            rank = jnp.cumsum(coming) - 1
            hit = coming[None, :] * (rank[None, :] == jnp.arange(slot_count)[:, None])
            anchor = jnp.sum(hit * jnp.arange(instances)[None, :], axis=1)
            got = jnp.take(got, anchor, axis=0)
        return got.reshape(slot_count * SEG, sent.shape[2])

    idx = jnp.tile(chosen, steps_t)[:, None]
    sent, idx = lax.optimization_barrier((sent, idx))
    values = move(sent)
    other_key, other_value, mine_key, mine_value, low = project(
        tokens.reshape(steps_t * requests, -1), key_matrix, value_matrix, adapter_down_maps, idx
    )
    swap = lambda a: lax.ppermute(a, "tp", [(0, 1), (1, 0)])
    valid = (jnp.arange(context)[None, :, None] < key_value_length.reshape(-1, 1, NB)).astype(
        jnp.int32
    )
    fresh, weights = weigh(
        queries,
        keys,
        valid.reshape(-1, 1, context * NB),
        (mine_key, mine_value),
        (swap(other_key), swap(other_value)),
        low,
        swap(low),
        idx,
        adapter_up_maps,
    )
    second = jnp.concatenate([fresh[t * requests : (t + 1) * requests] for t in range(steps_t)] + [weights], axis=1)
    second = jnp.dot(pick, second, preferred_element_type=jnp.float32).astype(jnp.bfloat16)
    second, values = lax.optimization_barrier((second, values))
    second = move(second)
    return serve(values, second, steps_t, width)


def solution(mesh):
    return jax.shard_map(
        on_device,
        mesh=mesh,
        in_specs=(
            P(None, ("grp", "inst"), "tp"),
            P(None, ("grp", "inst"), "tp"),
            P(("grp", "inst"), None, None, "tp"),
            P(("grp", "inst")),
            P(("grp", "inst"), None),
            P("grp"),
            P("tp", None),
            P("tp", None),
            P(("grp", "inst"), "tp", None),
            P(("grp", "inst"), None, None, "tp"),
        ),
        out_specs=(P(None, ("grp", "inst"), "tp"), P(None, ("grp", "inst"), None, "tp")),
        check_vma=False,
    )
```

```python
import functools

import jax
import jax.numpy as jnp
from jax import lax
from jax.experimental import pallas as pl
from jax.experimental.pallas import tpu as pltpu
from jax.sharding import PartitionSpec as P

QUERY_GROUP = 8
HEAD_SIZE = 128
SEG = 24
NB = 16
LANE = 16
PIECES = 4
VMEM_LIMIT = 56 * 1024 * 1024
F32 = jnp.float32
BF16 = jnp.bfloat16


def dot(a, b):
    return jnp.dot(a, b, preferred_element_type=F32)


def iota(shape, axis):
    return lax.broadcasted_iota(jnp.int32, shape, axis)


def fold_matrix(rows, n_of, p_base, lane_base):
    return (iota((rows, 128), 1) == lane_base + p_base + iota((rows, 128), 0) // n_of).astype(BF16)


def kernel(
    n, steps_t,
    leaving_ref, row_ref, col_ref, idx_ref, valid_ref,
    cache_hbm, tok_hbm, key_hbm, value_hbm, down_hbm, up_hbm, query_hbm,
    out_ref, kv_ref,
    cache, tok, key, value, down, up, query,
    pick_ref, vals, keys, sent_v, got_v, sent_s, got_s,
    part_k, part_v, got_k, got_vv, low_ref, got_low, fresh, wts,
    load_sem, piece_sem, pair_send, pair_recv, send_sem, recv_sem,
):
    me = lax.axis_index("inst")
    core = lax.axis_index("tp")
    requests = col_ref.shape[0]
    width = cache.shape[1]
    context = vals.shape[1] // width
    heads = width // HEAD_SIZE
    slots = down.shape[0]
    tile = key.shape[2]

    loads = [
        pltpu.make_async_copy(src, dst, load_sem.at[i])
        for i, (src, dst) in enumerate(
            [(cache_hbm, cache), (tok_hbm, tok), (down_hbm, down), (up_hbm, up), (query_hbm, query)]
        )
    ]
    pieces = []
    for j in range(PIECES):
        col = lax.rem((1 - core) * (PIECES // 2) + j, PIECES) * tile
        col = pl.multiple_of(col, tile)
        for i, (src, dst) in enumerate([(key_hbm, key), (value_hbm, value)]):
            pieces.append(
                pltpu.make_async_copy(src.at[:, pl.ds(col, tile)], dst.at[j], piece_sem.at[i, j])
            )
    loads[0].start()
    loads[1].start()
    for piece in pieces:
        piece.start()
    for load in loads[2:]:
        load.start()

    barrier = pltpu.get_barrier_semaphore()
    for k in range(1, n):
        pl.semaphore_signal(
            barrier, inc=1, device_id={"inst": lax.rem(me + k, n)},
            device_id_type=pl.DeviceIdType.MESH,
        )
    pl.semaphore_signal(
        barrier, inc=1, device_id={"tp": 1 - core}, device_id_type=pl.DeviceIdType.MESH
    )

    chosen = row_ref[...]
    r = iota((requests, requests), 0)
    c = iota((requests, requests), 1)
    same = jnp.where((col_ref[...] == chosen) & (r < c), 1, 0)
    seat = jnp.sum(same, axis=0, keepdims=True)
    for a in range(slots):
        seat += jnp.where(chosen == a, leaving_ref[a] * SEG, 0)
    pick_ref[...] = (iota((n * SEG, requests), 0) == seat).astype(BF16)

    block = 2 * context * NB
    r = iota((block // 2, block), 0)
    c = iota((block // 2, block), 1)
    first = (r % NB) * (2 * context) + (r // NB) * 2
    take_key = (c == first).astype(BF16)
    take_value = (c == first + 1).astype(BF16)
    loads[0].wait()

    def split(take, into):
        def body(b, carry):
            x = cache[pl.ds(pl.multiple_of(b * block, block), block)]
            v = dot(take, x).astype(BF16)
            here = pl.ds(pl.multiple_of(b * NB, NB), NB)
            for p in range(context):
                into[here, p * width : (p + 1) * width] = v[p * NB : (p + 1) * NB]
            return carry

        lax.fori_loop(0, requests // NB, body, 0)

    split(take_value, vals)
    pick = pick_ref[...]

    def place(rows, into, lanes):
        moved = dot(pick, rows)
        for d in range(n):
            into[d, :, lanes] = moved[d * SEG : (d + 1) * SEG].astype(BF16)

    for p in range(context):
        lanes = slice(p * width, (p + 1) * width)
        place(vals[:, lanes], sent_v, lanes)
    pl.semaphore_wait(barrier, n)

    def outgoing(i, k):
        src, dst = [(sent_v, got_v), (sent_s, got_s)][i]
        to = lax.rem(me + k, n)
        return pltpu.make_async_remote_copy(
            src_ref=src.at[to],
            dst_ref=dst.at[me],
            send_sem=send_sem.at[i, k],
            recv_sem=recv_sem.at[i, k],
            device_id={"inst": to},
            device_id_type=pl.DeviceIdType.MESH,
        )

    def incoming(i, k):
        src, dst = [(sent_v, got_v), (sent_s, got_s)][i]
        source = lax.rem(me - k + n, n)
        return pltpu.make_async_remote_copy(
            src_ref=src.at[source],
            dst_ref=dst.at[source],
            send_sem=send_sem.at[i, k],
            recv_sem=recv_sem.at[i, k],
            device_id={"inst": source},
            device_id_type=pl.DeviceIdType.MESH,
        )

    for k in range(1, n):
        outgoing(0, k).start()
    split(take_key, keys)

    loads[1].wait()

    def pair(i):
        src, dst = [(part_k.at[0 : PIECES // 2], got_k), (part_v.at[0 : PIECES // 2], got_vv), (low_ref, got_low)][i]
        return pltpu.make_async_remote_copy(
            src_ref=src,
            dst_ref=dst,
            send_sem=pair_send.at[i],
            recv_sem=pair_recv.at[i],
            device_id={"tp": 1 - core},
            device_id_type=pl.DeviceIdType.MESH,
        )

    for j in range(PIECES):
        pieces[2 * j].wait()
        part_k[j] = dot(tok[...], key[j])
        pieces[2 * j + 1].wait()
        part_v[j] = dot(tok[...], value[j])
        if j == PIECES // 2 - 1:
            pair(0).start()
            pair(1).start()
            loads[2].wait()
            low_ref[...] = jnp.zeros_like(low_ref)

            def add_low(a, carry):
                low = dot(tok[...], down[a])
                low_ref[...] = jnp.where(idx_ref[...] == a, low, low_ref[...])
                return carry

            lax.fori_loop(0, slots, add_low, 0)
            pair(2).start()
    loads[3].wait()
    for i in range(3):
        pair(i).wait()
    low = (low_ref[...] + got_low[...]).astype(BF16)
    rank = low.shape[1] // 2
    idx = idx_ref[...]
    parts = [jnp.where(idx == s, low, jnp.zeros_like(low)) for s in range(slots)]
    for kind, (mine, got) in enumerate([(part_k, got_k), (part_v, got_vv)]):
        for j in range(PIECES // 2):
            total = mine[PIECES // 2 + j] + got[j]
            for s in range(slots):
                total += dot(
                    parts[s][:, kind * rank : (kind + 1) * rank],
                    up[s, kind, :, j * tile : (j + 1) * tile],
                )
            start = kind * width + j * tile
            fresh[:, start : start + tile] = total.astype(BF16)

    rows = QUERY_GROUP * steps_t * NB
    half = rows // 2
    old_lanes = context * NB
    new_lanes = steps_t * NB
    factor = HEAD_SIZE ** (-0.5)
    dims = (((1,), (1,)), ((), ()))
    loads[4].wait()

    def weigh(b, carry):
        here = pl.ds(pl.multiple_of(b * NB, NB), NB)
        row, lane = iota((rows, old_lanes), 0), iota((rows, old_lanes), 1)
        old_ok = (row % NB == lane % NB) & (valid_ref[b] > 0)
        row, lane = iota((rows, new_lanes), 0), iota((rows, new_lanes), 1)
        new_ok = (row % NB == lane % NB) & (lane // NB <= (row // NB) % steps_t)
        q = query[:, here, :].reshape(steps_t * NB, query.shape[2])
        k = keys[here, :]
        new_k = jnp.concatenate(
            [
                fresh[pl.ds(pl.multiple_of(t * requests + b * NB, NB), NB), :width]
                for t in range(steps_t)
            ],
            axis=0,
        )
        total = jnp.zeros((half, 128), F32)
        for g in range(heads):
            start = g * QUERY_GROUP * HEAD_SIZE
            qg = jnp.concatenate(
                [q[:, start + h * HEAD_SIZE : start + (h + 1) * HEAD_SIZE] for h in range(QUERY_GROUP)],
                axis=0,
            )
            at = g * HEAD_SIZE
            kg = jnp.concatenate(
                [k[:, p * width + at : p * width + at + HEAD_SIZE] for p in range(context)], axis=0
            )
            ng = new_k[:, at : at + HEAD_SIZE]
            old = lax.dot_general(qg, kg, dims, preferred_element_type=F32) * factor
            new = lax.dot_general(qg, ng, dims, preferred_element_type=F32) * factor
            old = jnp.where(old_ok, old, -jnp.inf)
            new = jnp.where(new_ok, new, -jnp.inf)
            top = jnp.maximum(
                jnp.max(old, axis=1, keepdims=True), jnp.max(new, axis=1, keepdims=True)
            )
            old = jnp.exp(old - top)
            new = jnp.exp(new - top)
            norm = jnp.sum(old, axis=1, keepdims=True) + jnp.sum(new, axis=1, keepdims=True)
            scale = 1.0 / norm
            old = (old * scale).astype(BF16)
            new = (new * scale).astype(BF16)
            for part in range(2):
                base = part * 64 + g * LANE
                span = slice(part * half, (part + 1) * half)
                total += dot(old[span], fold_matrix(old_lanes, NB, 0, base))
                total += dot(new[span], fold_matrix(new_lanes, NB, context, base))
        total = total.astype(BF16)
        for i in range(half // NB):
            wts[here, i * 128 : (i + 1) * 128] = total[i * NB : (i + 1) * NB]
        return carry

    lax.fori_loop(0, requests // NB, weigh, 0)

    chunk = 2 * width
    for t in range(steps_t):
        place(
            fresh[t * requests : (t + 1) * requests, :], sent_s, slice(t * chunk, (t + 1) * chunk)
        )
    place(wts[...], sent_s, slice(steps_t * chunk, steps_t * chunk + wts.shape[1]))
    for k in range(1, n):
        outgoing(1, k).start()

    rows = QUERY_GROUP * steps_t * SEG
    lanes = (context + steps_t) * SEG

    def serve(v_ref, s_ref, source):
        own = iota((rows, lanes), 0) % SEG == iota((rows, lanes), 1) % SEG
        spread_r = iota((128, lanes), 0)
        spread_c = iota((128, lanes), 1) // SEG
        v = v_ref[source].astype(F32)
        s = s_ref[source].astype(F32)
        w = [
            s[:, steps_t * chunk + i * 128 : steps_t * chunk + (i + 1) * 128]
            for i in range(QUERY_GROUP * steps_t // 2)
        ]
        w = jnp.concatenate(w, axis=0).astype(BF16)
        r2, c2 = iota((2 * SEG, 2 * SEG), 0), iota((2 * SEG, 2 * SEG), 1)
        weave = (c2 == (r2 % 2) * SEG + r2 // 2).astype(BF16)
        for t in range(steps_t):
            both = [s[:, t * chunk + i * width : t * chunk + (i + 1) * width] for i in range(2)]
            both = dot(weave, jnp.concatenate(both, axis=0).astype(BF16))
            kv_ref[t, source] = both.reshape(SEG, 2, width).astype(BF16)
        for g in range(heads):
            at = g * HEAD_SIZE
            vg = [v[:, p * width + at : p * width + at + HEAD_SIZE] for p in range(context)]
            for t in range(steps_t):
                start = t * chunk + width + at
                vg.append(s[:, start : start + HEAD_SIZE])
            vg = jnp.concatenate(vg, axis=0).astype(BF16)
            wide = []
            for part in range(2):
                spread = (spread_r == part * 64 + g * LANE + spread_c).astype(BF16)
                wide.append(dot(w, spread))
            wide = jnp.where(own, jnp.concatenate(wide, axis=0), 0.0).astype(BF16)
            res = dot(wide, vg)
            for h in range(QUERY_GROUP):
                start = (g * QUERY_GROUP + h) * HEAD_SIZE
                for t in range(steps_t):
                    at_row = (h * steps_t + t) * SEG
                    out_ref[t, source, :, start : start + HEAD_SIZE] = res[
                        at_row : at_row + SEG
                    ].astype(BF16)

    serve(sent_v, sent_s, me)

    def arrive(k):
        incoming(0, k).wait_recv()
        incoming(1, k).wait_recv()
        serve(got_v, got_s, lax.rem(me - k + n, n))

    def step(k, carry):
        arrive(k)
        return carry

    lax.fori_loop(1, n, step, 0)
    for i in range(2):
        for k in range(1, n):
            outgoing(i, k).wait_send()


def on_device(
    tokens,
    queries,
    key_value_cache,
    key_value_length,
    request_adapter_index,
    adapter_destination,
    key_matrix,
    value_matrix,
    adapter_down_maps,
    adapter_up_maps,
):
    slots, depth, rank = adapter_down_maps.shape
    requests = request_adapter_index.shape[0]
    steps_t = tokens.shape[0]
    rows = steps_t * requests
    _, context, _, width = key_value_cache.shape
    query_width = queries.shape[2]
    n = lax.axis_size("inst")
    own_index = lax.axis_index("inst")
    chosen = request_adapter_index[:, 0]
    leaving = lax.dynamic_slice_in_dim(adapter_destination, own_index * slots, slots)
    valid = jnp.arange(context)[None, :, None] < key_value_length.reshape(-1, 1, NB)
    valid = valid.astype(jnp.int32).reshape(-1, 1, context * NB)
    idx = jnp.tile(chosen, steps_t)[:, None]
    packed = QUERY_GROUP * steps_t // 2 * 128
    second = steps_t * 2 * width + packed
    tile = key_matrix.shape[1] // PIECES
    vmem = pl.BlockSpec(memory_space=pltpu.VMEM)
    hbm = pl.BlockSpec(memory_space=pl.ANY)
    dma = pltpu.SemaphoreType.DMA
    attended, new_kv = pl.pallas_call(
        functools.partial(kernel, n, steps_t),
        in_specs=[pl.BlockSpec(memory_space=pltpu.SMEM)] + [vmem] * 4 + [hbm] * 7,
        out_specs=[vmem, vmem],
        out_shape=[
            jax.ShapeDtypeStruct((steps_t, n, SEG, query_width), BF16),
            jax.ShapeDtypeStruct((steps_t, n, SEG, 2, width), BF16),
        ],
        scratch_shapes=[
            pltpu.VMEM((requests * context * 2, width), BF16),
            pltpu.VMEM((rows, depth), BF16),
            pltpu.VMEM((PIECES, depth, tile), BF16),
            pltpu.VMEM((PIECES, depth, tile), BF16),
            pltpu.VMEM(adapter_down_maps.shape, BF16),
            pltpu.VMEM(adapter_up_maps.shape, BF16),
            pltpu.VMEM(queries.shape, BF16),
            pltpu.VMEM((n * SEG, requests), BF16),
            pltpu.VMEM((requests, context * width), BF16),
            pltpu.VMEM((requests, context * width), BF16),
            pltpu.VMEM((n, SEG, context * width), BF16),
            pltpu.VMEM((n, SEG, context * width), BF16),
            pltpu.VMEM((n, SEG, second), BF16),
            pltpu.VMEM((n, SEG, second), BF16),
            pltpu.VMEM((PIECES, rows, tile), F32),
            pltpu.VMEM((PIECES, rows, tile), F32),
            pltpu.VMEM((PIECES // 2, rows, tile), F32),
            pltpu.VMEM((PIECES // 2, rows, tile), F32),
            pltpu.VMEM((rows, rank), F32),
            pltpu.VMEM((rows, rank), F32),
            pltpu.VMEM((rows, 2 * width), BF16),
            pltpu.VMEM((requests, packed), BF16),
            dma((5,)),
            dma((2, PIECES)),
            dma((3,)),
            dma((3,)),
            dma((2, n)),
            dma((2, n)),
        ],
        compiler_params=pltpu.CompilerParams(
            collective_id=0, has_side_effects=True, vmem_limit_bytes=VMEM_LIMIT
        ),
        name="migrate",
    )(
        leaving, chosen[None, :], chosen[:, None], idx, valid,
        key_value_cache.reshape(-1, width), tokens.reshape(rows, depth), key_matrix, value_matrix,
        adapter_down_maps, adapter_up_maps, queries,
    )
    if n != slots:
        coming = adapter_destination.reshape(n, slots) == own_index
        coming = jnp.sum(coming.astype(jnp.int32), axis=1)
        hit = coming[None, :] * (jnp.cumsum(coming)[None, :] - 1 == jnp.arange(slots)[:, None])
        anchor = jnp.sum(hit * jnp.arange(n)[None, :], axis=1)
        attended = jnp.take(attended, anchor, axis=1)
        new_kv = jnp.take(new_kv, anchor, axis=1)
    return (
        attended.reshape(steps_t, slots * SEG, query_width),
        new_kv.reshape(steps_t, slots * SEG, 2, width),
    )


def solution(mesh):
    return jax.shard_map(
        on_device,
        mesh=mesh,
        in_specs=(
            P(None, ("grp", "inst"), "tp"),
            P(None, ("grp", "inst"), "tp"),
            P(("grp", "inst"), None, None, "tp"),
            P(("grp", "inst")),
            P(("grp", "inst"), None),
            P("grp"),
            P("tp", None),
            P("tp", None),
            P(("grp", "inst"), "tp", None),
            P(("grp", "inst"), None, None, "tp"),
        ),
        out_specs=(P(None, ("grp", "inst"), "tp"), P(None, ("grp", "inst"), None, "tp")),
        check_vma=False,
    )
```

```python
import functools

import jax
import jax.numpy as jnp
from jax import lax
from jax.experimental import pallas as pl
from jax.experimental.pallas import tpu as pltpu
from jax.sharding import PartitionSpec as P

QUERY_GROUP = 8
HEAD_SIZE = 128
SEG = 24
NB = 16
LANE = 16
PIECES = 4
MIB = 1024 * 1024
F32 = jnp.float32
BF16 = jnp.bfloat16


def dot(a, b):
    return jnp.dot(a, b, preferred_element_type=F32)


def iota(shape, axis):
    return lax.broadcasted_iota(jnp.int32, shape, axis)


def fold_matrix(rows, n_of, p_base, lane_base):
    return (iota((rows, 128), 1) == lane_base + p_base + iota((rows, 128), 0) // n_of).astype(BF16)


def kernel(
    n, steps_t,
    leaving_ref, row_ref, length_ref,
    cache_hbm, tok_hbm, key_hbm, value_hbm, down_hbm, up_hbm, query_hbm,
    out_ref, kv_ref,
    cache, tok, key, value, down, up, query,
    pick_ref, vals, keys, sent_v, got_v, sent_s, got_s,
    part_k, part_v, got_k, got_vv, low_ref, got_low, fresh, wts,
    idx_ref, len_ref, load_sem, piece_sem, pair_send, pair_recv, send_sem, recv_sem,
):
    me = lax.axis_index("inst")
    core = lax.axis_index("tp")
    requests, _, _, width = cache.shape
    context = vals.shape[1] // width
    heads = width // HEAD_SIZE
    slots = down.shape[0]
    tile = key.shape[2]

    loads = [
        pltpu.make_async_copy(src, dst, load_sem.at[i])
        for i, (src, dst) in enumerate(
            [(cache_hbm, cache), (tok_hbm, tok), (down_hbm, down), (up_hbm, up), (query_hbm, query)]
        )
    ]
    pieces = []
    for j in range(PIECES):
        col = lax.rem((1 - core) * (PIECES // 2) + j, PIECES) * tile
        col = pl.multiple_of(col, tile)
        for i, (src, dst) in enumerate([(key_hbm, key), (value_hbm, value)]):
            pieces.append(
                pltpu.make_async_copy(src.at[:, pl.ds(col, tile)], dst.at[j], piece_sem.at[i, j])
            )
    loads[0].start()
    loads[1].start()
    for piece in pieces:
        piece.start()
    for load in loads[2:]:
        load.start()

    def partner(k):
        total, bit = 0, 1
        while bit < n:
            total += lax.rem(me // bit + k // bit, 2) * bit
            bit *= 2
        return total

    barrier = pltpu.get_barrier_semaphore()
    for k in range(1, n):
        pl.semaphore_signal(
            barrier, inc=1, device_id={"inst": partner(k)},
            device_id_type=pl.DeviceIdType.MESH,
        )
    pl.semaphore_signal(
        barrier, inc=1, device_id={"tp": 1 - core}, device_id_type=pl.DeviceIdType.MESH
    )

    chosen = row_ref[...]
    r = iota((requests, requests), 0)
    c = iota((requests, requests), 1)
    column = jnp.sum(jnp.where(r == c, chosen, 0), axis=1, keepdims=True)
    for t in range(steps_t):
        idx_ref[t * requests : (t + 1) * requests] = column
    len_ref[...] = jnp.sum(jnp.where(r == c, length_ref[...], 0), axis=1, keepdims=True)
    same = jnp.where((column == chosen) & (r < c), 1, 0)
    seat = jnp.sum(same, axis=0, keepdims=True)
    for a in range(slots):
        seat += jnp.where(chosen == a, leaving_ref[me * slots + a] * SEG, 0)
    pick_ref[...] = (iota((n * SEG, requests), 0) == seat).astype(BF16)

    block = 2 * context * NB
    r = iota((block // 2, block), 0)
    c = iota((block // 2, block), 1)
    first = (r % NB) * (2 * context) + (r // NB) * 2
    take_key = (c == first).astype(BF16)
    take_value = (c == first + 1).astype(BF16)
    loads[0].wait()

    def split(take, into):
        def body(b, carry):
            x = cache[pl.ds(b * NB, NB)].reshape(block, width)
            v = dot(take, x).astype(BF16)
            here = pl.ds(pl.multiple_of(b * NB, NB), NB)
            for p in range(context):
                into[here, p * width : (p + 1) * width] = v[p * NB : (p + 1) * NB]
            return carry

        lax.fori_loop(0, requests // NB, body, 0)

    split(take_value, vals)
    pick = pick_ref[...]

    def place(rows, into, lanes):
        moved = dot(pick, rows)
        for d in range(n):
            into[d, :, lanes] = moved[d * SEG : (d + 1) * SEG].astype(BF16)

    for p in range(context):
        lanes = slice(p * width, (p + 1) * width)
        place(vals[:, lanes], sent_v, lanes)
    pl.semaphore_wait(barrier, n)

    def outgoing(i, k):
        src, dst = [(sent_v, got_v), (sent_s, got_s)][i]
        to = partner(k)
        return pltpu.make_async_remote_copy(
            src_ref=src.at[to],
            dst_ref=dst.at[me],
            send_sem=send_sem.at[i, k],
            recv_sem=recv_sem.at[i, k],
            device_id={"inst": to},
            device_id_type=pl.DeviceIdType.MESH,
        )

    def incoming(i, k):
        src, dst = [(sent_v, got_v), (sent_s, got_s)][i]
        source = partner(k)
        return pltpu.make_async_remote_copy(
            src_ref=src.at[source],
            dst_ref=dst.at[source],
            send_sem=send_sem.at[i, k],
            recv_sem=recv_sem.at[i, k],
            device_id={"inst": source},
            device_id_type=pl.DeviceIdType.MESH,
        )

    turn = n // 2 - lax.rem(me // 2, 2) * 2 - core

    def send(i):
        def one(j, carry):
            m = lax.rem(j + turn, n - 1)
            outgoing(i, lax.rem(n // 2 + m + m // (n // 2), n)).start()
            return carry

        lax.fori_loop(0, n - 1, one, 0)

    send(0)
    split(take_key, keys)

    loads[1].wait()

    def pair(i):
        src, dst = [(part_k.at[0 : PIECES // 2], got_k), (part_v.at[0 : PIECES // 2], got_vv), (low_ref, got_low)][i]
        return pltpu.make_async_remote_copy(
            src_ref=src,
            dst_ref=dst,
            send_sem=pair_send.at[i],
            recv_sem=pair_recv.at[i],
            device_id={"tp": 1 - core},
            device_id_type=pl.DeviceIdType.MESH,
        )

    for j in range(PIECES):
        pieces[2 * j].wait()
        part_k[j] = dot(tok[...], key[j])
        pieces[2 * j + 1].wait()
        part_v[j] = dot(tok[...], value[j])
        if j == PIECES // 2 - 1:
            pair(0).start()
            pair(1).start()
            loads[2].wait()
            low_ref[...] = jnp.zeros_like(low_ref)

            def add_low(a, carry):
                low = dot(tok[...], down[a])
                low_ref[...] = jnp.where(idx_ref[...] == a, low, low_ref[...])
                return carry

            lax.fori_loop(0, slots, add_low, 0)
            pair(2).start()
    loads[3].wait()
    for i in range(3):
        pair(i).wait()
    low = (low_ref[...] + got_low[...]).astype(BF16)
    rank = low.shape[1] // 2
    idx = idx_ref[...]
    parts = [jnp.where(idx == s, low, jnp.zeros_like(low)) for s in range(slots)]
    for kind, (mine, got) in enumerate([(part_k, got_k), (part_v, got_vv)]):
        for j in range(PIECES // 2):
            total = mine[PIECES // 2 + j] + got[j]
            for s in range(slots):
                total += dot(
                    parts[s][:, kind * rank : (kind + 1) * rank],
                    up[s, kind, :, j * tile : (j + 1) * tile],
                )
            start = kind * width + j * tile
            fresh[:, start : start + tile] = total.astype(BF16)

    rows = QUERY_GROUP * steps_t * NB
    half = rows // 2
    old_lanes = context * NB
    new_lanes = steps_t * NB
    factor = HEAD_SIZE ** (-0.5)
    dims = (((1,), (1,)), ((), ()))
    loads[4].wait()

    def weigh(b, carry):
        here = pl.ds(pl.multiple_of(b * NB, NB), NB)
        row, lane = iota((rows, old_lanes), 0), iota((rows, old_lanes), 1)
        live = jnp.concatenate([len_ref[here, :]] * (QUERY_GROUP * steps_t), axis=0)
        old_ok = (row % NB == lane % NB) & (lane // NB < live)
        row, lane = iota((rows, new_lanes), 0), iota((rows, new_lanes), 1)
        new_ok = (row % NB == lane % NB) & (lane // NB <= (row // NB) % steps_t)
        q = query[:, here, :].reshape(steps_t * NB, query.shape[2])
        k = keys[here, :]
        new_k = jnp.concatenate(
            [
                fresh[pl.ds(pl.multiple_of(t * requests + b * NB, NB), NB), :width]
                for t in range(steps_t)
            ],
            axis=0,
        )
        total = jnp.zeros((half, 128), F32)
        for g in range(heads):
            start = g * QUERY_GROUP * HEAD_SIZE
            qg = jnp.concatenate(
                [q[:, start + h * HEAD_SIZE : start + (h + 1) * HEAD_SIZE] for h in range(QUERY_GROUP)],
                axis=0,
            )
            at = g * HEAD_SIZE
            kg = jnp.concatenate(
                [k[:, p * width + at : p * width + at + HEAD_SIZE] for p in range(context)], axis=0
            )
            ng = new_k[:, at : at + HEAD_SIZE]
            old = lax.dot_general(qg, kg, dims, preferred_element_type=F32) * factor
            new = lax.dot_general(qg, ng, dims, preferred_element_type=F32) * factor
            old = jnp.where(old_ok, old, -jnp.inf)
            new = jnp.where(new_ok, new, -jnp.inf)
            top = jnp.maximum(
                jnp.max(old, axis=1, keepdims=True), jnp.max(new, axis=1, keepdims=True)
            )
            old = jnp.exp(old - top)
            new = jnp.exp(new - top)
            norm = jnp.sum(old, axis=1, keepdims=True) + jnp.sum(new, axis=1, keepdims=True)
            scale = 1.0 / norm
            old = (old * scale).astype(BF16)
            new = (new * scale).astype(BF16)
            for part in range(2):
                base = part * 64 + g * LANE
                span = slice(part * half, (part + 1) * half)
                total += dot(old[span], fold_matrix(old_lanes, NB, 0, base))
                total += dot(new[span], fold_matrix(new_lanes, NB, context, base))
        total = total.astype(BF16)
        for i in range(half // NB):
            wts[here, i * 128 : (i + 1) * 128] = total[i * NB : (i + 1) * NB]
        return carry

    lax.fori_loop(0, requests // NB, weigh, 0)

    chunk = 2 * width
    for t in range(steps_t):
        place(
            fresh[t * requests : (t + 1) * requests, :], sent_s, slice(t * chunk, (t + 1) * chunk)
        )
    place(wts[...], sent_s, slice(steps_t * chunk, steps_t * chunk + wts.shape[1]))
    send(1)

    rows = QUERY_GROUP * steps_t * SEG
    lanes = (context + steps_t) * SEG

    def serve(v_ref, s_ref, source):
        own = iota((rows, lanes), 0) % SEG == iota((rows, lanes), 1) % SEG
        spread_r = iota((128, lanes), 0)
        spread_c = iota((128, lanes), 1) // SEG
        v = v_ref[source].astype(F32)
        s = s_ref[source].astype(F32)
        w = [
            s[:, steps_t * chunk + i * 128 : steps_t * chunk + (i + 1) * 128]
            for i in range(QUERY_GROUP * steps_t // 2)
        ]
        w = jnp.concatenate(w, axis=0).astype(BF16)
        r2, c2 = iota((2 * SEG, 2 * SEG), 0), iota((2 * SEG, 2 * SEG), 1)
        weave = (c2 == (r2 % 2) * SEG + r2 // 2).astype(BF16)
        for t in range(steps_t):
            both = [s[:, t * chunk + i * width : t * chunk + (i + 1) * width] for i in range(2)]
            both = dot(weave, jnp.concatenate(both, axis=0).astype(BF16))
            kv_ref[t, source] = both.reshape(SEG, 2, width).astype(BF16)
        for g in range(heads):
            at = g * HEAD_SIZE
            vg = [v[:, p * width + at : p * width + at + HEAD_SIZE] for p in range(context)]
            for t in range(steps_t):
                start = t * chunk + width + at
                vg.append(s[:, start : start + HEAD_SIZE])
            vg = jnp.concatenate(vg, axis=0).astype(BF16)
            wide = []
            for part in range(2):
                spread = (spread_r == part * 64 + g * LANE + spread_c).astype(BF16)
                wide.append(dot(w, spread))
            wide = jnp.where(own, jnp.concatenate(wide, axis=0), 0.0).astype(BF16)
            res = dot(wide, vg)
            for h in range(QUERY_GROUP):
                start = (g * QUERY_GROUP + h) * HEAD_SIZE
                for t in range(steps_t):
                    at_row = (h * steps_t + t) * SEG
                    out_ref[t, source, :, start : start + HEAD_SIZE] = res[
                        at_row : at_row + SEG
                    ].astype(BF16)

    serve(sent_v, sent_s, me)

    def arrive(k):
        incoming(0, k).wait_recv()
        incoming(1, k).wait_recv()
        serve(got_v, got_s, partner(k))

    def step(k, carry):
        arrive(k)
        return carry

    lax.fori_loop(1, n, step, 0)
    for i in range(2):
        for k in range(1, n):
            outgoing(i, k).wait_send()


def on_device(
    tokens,
    queries,
    key_value_cache,
    key_value_length,
    request_adapter_index,
    adapter_destination,
    key_matrix,
    value_matrix,
    adapter_down_maps,
    adapter_up_maps,
):
    slots, depth, rank = adapter_down_maps.shape
    requests = request_adapter_index.shape[0]
    steps_t = tokens.shape[0]
    rows = steps_t * requests
    _, context, _, width = key_value_cache.shape
    query_width = queries.shape[2]
    n = lax.axis_size("inst")
    packed = QUERY_GROUP * steps_t // 2 * 128
    second = steps_t * 2 * width + packed
    tile = key_matrix.shape[1] // PIECES
    vmem = pl.BlockSpec(memory_space=pltpu.VMEM)
    hbm = pl.BlockSpec(memory_space=pltpu.MemorySpace.HBM)
    dma = pltpu.SemaphoreType.DMA
    attended, new_kv = pl.pallas_call(
        functools.partial(kernel, n, steps_t),
        in_specs=[pl.BlockSpec(memory_space=pltpu.SMEM)] + [vmem] * 2 + [hbm] * 7,
        out_specs=[vmem, vmem],
        out_shape=[
            jax.ShapeDtypeStruct((steps_t, n, SEG, query_width), BF16),
            jax.ShapeDtypeStruct((steps_t, n, SEG, 2, width), BF16),
        ],
        scratch_shapes=[
            pltpu.VMEM(key_value_cache.shape, BF16),
            pltpu.VMEM((rows, depth), BF16),
            pltpu.VMEM((PIECES, depth, tile), BF16),
            pltpu.VMEM((PIECES, depth, tile), BF16),
            pltpu.VMEM(adapter_down_maps.shape, BF16),
            pltpu.VMEM(adapter_up_maps.shape, BF16),
            pltpu.VMEM(queries.shape, BF16),
            pltpu.VMEM((n * SEG, requests), BF16),
            pltpu.VMEM((requests, context * width), BF16),
            pltpu.VMEM((requests, context * width), BF16),
            pltpu.VMEM((n, SEG, context * width), BF16),
            pltpu.VMEM((n, SEG, context * width), BF16),
            pltpu.VMEM((n, SEG, second), BF16),
            pltpu.VMEM((n, SEG, second), BF16),
            pltpu.VMEM((PIECES, rows, tile), F32),
            pltpu.VMEM((PIECES, rows, tile), F32),
            pltpu.VMEM((PIECES // 2, rows, tile), F32),
            pltpu.VMEM((PIECES // 2, rows, tile), F32),
            pltpu.VMEM((rows, rank), F32),
            pltpu.VMEM((rows, rank), F32),
            pltpu.VMEM((rows, 2 * width), BF16),
            pltpu.VMEM((requests, packed), BF16),
            pltpu.VMEM((rows, 1), jnp.int32),
            pltpu.VMEM((requests, 1), jnp.int32),
            dma((5,)),
            dma((2, PIECES)),
            dma((3,)),
            dma((3,)),
            dma((2, n)),
            dma((2, n)),
        ],
        compiler_params=pltpu.CompilerParams(
            collective_id=0, has_side_effects=True, vmem_limit_bytes=(32 + n) * MIB
        ),
        name="migrate",
    )(
        adapter_destination, request_adapter_index.reshape(1, requests),
        key_value_length.reshape(1, requests), key_value_cache, tokens.reshape(rows, depth), key_matrix, value_matrix,
        adapter_down_maps, adapter_up_maps, queries,
    )
    if n != slots:
        coming = adapter_destination.reshape(n, slots) == lax.axis_index("inst")
        coming = jnp.sum(coming.astype(jnp.int32), axis=1)
        hit = coming[None, :] * (jnp.cumsum(coming)[None, :] - 1 == jnp.arange(slots)[:, None])
        anchor = jnp.sum(hit * jnp.arange(n)[None, :], axis=1)
        attended = jnp.take(attended, anchor, axis=1)
        new_kv = jnp.take(new_kv, anchor, axis=1)
    return (
        attended.reshape(steps_t, slots * SEG, query_width),
        new_kv.reshape(steps_t, slots * SEG, 2, width),
    )


def solution(mesh):
    return jax.shard_map(
        on_device,
        mesh=mesh,
        in_specs=(
            P(None, ("grp", "inst"), "tp"),
            P(None, ("grp", "inst"), "tp"),
            P(("grp", "inst"), None, None, "tp"),
            P(("grp", "inst")),
            P(("grp", "inst"), None),
            P("grp"),
            P("tp", None),
            P("tp", None),
            P(("grp", "inst"), "tp", None),
            P(("grp", "inst"), None, None, "tp"),
        ),
        out_specs=(P(None, ("grp", "inst"), "tp"), P(None, ("grp", "inst"), None, "tp")),
        check_vma=False,
    )
```

```python
import functools

import jax
import jax.numpy as jnp
from jax import lax
from jax.experimental import pallas as pl
from jax.experimental.pallas import tpu as pltpu
from jax.sharding import PartitionSpec as P

QUERY_GROUP = 8
HEAD_SIZE = 128
SEG = 24
NB = 16
PIECES = 4
MIB = 1024 * 1024
F32 = jnp.float32
BF16 = jnp.bfloat16


def dot(a, b):
    return jnp.dot(a, b, preferred_element_type=F32)


def iota(shape, axis):
    return lax.broadcasted_iota(jnp.int32, shape, axis)


def kernel(
    n, steps_t,
    leaving_ref, row_ref, length_ref,
    cache_hbm, tok_hbm, key_hbm, value_hbm, down_hbm, up_hbm, query_hbm,
    out_ref, kv_ref,
    cache, tok, key, value, down, up, query,
    pick_ref, vals, keys, sent_v, got_v, sent_s, got_s,
    part_k, part_v, got_k, got_vv, low_ref, got_low, fresh, wts,
    idx_ref, len_ref, load_sem, piece_sem, pair_send, pair_recv, send_sem, recv_sem,
):
    me = lax.axis_index("inst")
    core = lax.axis_index("tp")
    requests, _, _, width = cache.shape
    context = vals.shape[1] // width
    heads = width // HEAD_SIZE
    slots = down.shape[0]
    tile = key.shape[2]

    loads = [
        pltpu.make_async_copy(src, dst, load_sem.at[i])
        for i, (src, dst) in enumerate(
            [(cache_hbm, cache), (tok_hbm, tok), (down_hbm, down), (up_hbm, up), (query_hbm, query)]
        )
    ]
    pieces = []
    for j in range(PIECES):
        col = lax.rem((1 - core) * (PIECES // 2) + j, PIECES) * tile
        col = pl.multiple_of(col, tile)
        for i, (src, dst) in enumerate([(key_hbm, key), (value_hbm, value)]):
            pieces.append(
                pltpu.make_async_copy(src.at[:, pl.ds(col, tile)], dst.at[j], piece_sem.at[i, j])
            )
    loads[0].start()
    loads[1].start()
    for piece in pieces:
        piece.start()
    for load in loads[2:]:
        load.start()

    def partner(k):
        total, bit = 0, 1
        while bit < n:
            total += lax.rem(me // bit + k // bit, 2) * bit
            bit *= 2
        return total

    barrier = pltpu.get_barrier_semaphore()
    for k in range(1, n):
        pl.semaphore_signal(
            barrier, inc=1, device_id={"inst": partner(k)},
            device_id_type=pl.DeviceIdType.MESH,
        )
    pl.semaphore_signal(
        barrier, inc=1, device_id={"tp": 1 - core}, device_id_type=pl.DeviceIdType.MESH
    )

    chosen = row_ref[...]
    r = iota((requests, requests), 0)
    c = iota((requests, requests), 1)
    column = jnp.sum(jnp.where(r == c, chosen, 0), axis=1, keepdims=True)
    for t in range(steps_t):
        idx_ref[t * requests : (t + 1) * requests] = column
    len_ref[...] = jnp.sum(jnp.where(r == c, length_ref[...], 0), axis=1, keepdims=True)
    same = jnp.where((column == chosen) & (r < c), 1, 0)
    seat = jnp.sum(same, axis=0, keepdims=True)
    for a in range(slots):
        seat += jnp.where(chosen == a, leaving_ref[me * slots + a] * SEG, 0)
    pick_ref[...] = (iota((n * SEG, requests), 0) == seat).astype(BF16)

    block = 2 * context * NB
    r = iota((block // 2, block), 0)
    c = iota((block // 2, block), 1)
    first = (r % NB) * (2 * context) + (r // NB) * 2
    take_key = (c == first).astype(BF16)
    take_value = (c == first + 1).astype(BF16)
    loads[0].wait()

    def split(take, into):
        def body(b, carry):
            x = cache[pl.ds(b * NB, NB)].reshape(block, width)
            v = dot(take, x).astype(BF16)
            here = pl.ds(pl.multiple_of(b * NB, NB), NB)
            for p in range(context):
                into[here, p * width : (p + 1) * width] = v[p * NB : (p + 1) * NB]
            return carry

        lax.fori_loop(0, requests // NB, body, 0)

    split(take_value, vals)
    pick = pick_ref[...]

    def place(rows, into, lanes):
        moved = dot(pick, rows)
        for d in range(n):
            into[d, :, lanes] = moved[d * SEG : (d + 1) * SEG].astype(BF16)

    for p in range(context):
        lanes = slice(p * width, (p + 1) * width)
        place(vals[:, lanes], sent_v, lanes)
    pl.semaphore_wait(barrier, n)

    def outgoing(i, k):
        src, dst = [(sent_v, got_v), (sent_s, got_s)][i]
        to = partner(k)
        return pltpu.make_async_remote_copy(
            src_ref=src.at[to],
            dst_ref=dst.at[me],
            send_sem=send_sem.at[i, k],
            recv_sem=recv_sem.at[i, k],
            device_id={"inst": to},
            device_id_type=pl.DeviceIdType.MESH,
        )

    def incoming(i, k):
        src, dst = [(sent_v, got_v), (sent_s, got_s)][i]
        source = partner(k)
        return pltpu.make_async_remote_copy(
            src_ref=src.at[source],
            dst_ref=dst.at[source],
            send_sem=send_sem.at[i, k],
            recv_sem=recv_sem.at[i, k],
            device_id={"inst": source},
            device_id_type=pl.DeviceIdType.MESH,
        )

    turn = n // 2 - lax.rem(me // 2, 2) * 2 - core

    def send(i):
        def one(j, carry):
            m = lax.rem(j + turn, n - 1)
            outgoing(i, lax.rem(n // 2 + m + m // (n // 2), n)).start()
            return carry

        lax.fori_loop(0, n - 1, one, 0)

    send(0)
    split(take_key, keys)

    loads[1].wait()

    def pair(i):
        src, dst = [(part_k.at[0 : PIECES // 2], got_k), (part_v.at[0 : PIECES // 2], got_vv), (low_ref, got_low)][i]
        return pltpu.make_async_remote_copy(
            src_ref=src,
            dst_ref=dst,
            send_sem=pair_send.at[i],
            recv_sem=pair_recv.at[i],
            device_id={"tp": 1 - core},
            device_id_type=pl.DeviceIdType.MESH,
        )

    for j in range(PIECES):
        pieces[2 * j].wait()
        part_k[j] = dot(tok[...], key[j])
        pieces[2 * j + 1].wait()
        part_v[j] = dot(tok[...], value[j])
        if j == PIECES // 2 - 1:
            pair(0).start()
            pair(1).start()
            loads[2].wait()
            low_ref[...] = jnp.zeros_like(low_ref)

            def add_low(a, carry):
                low = dot(tok[...], down[a])
                low_ref[...] = jnp.where(idx_ref[...] == a, low, low_ref[...])
                return carry

            lax.fori_loop(0, slots, add_low, 0)
            pair(2).start()
    loads[3].wait()
    for i in range(3):
        pair(i).wait()
    low = (low_ref[...] + got_low[...]).astype(BF16)
    rank = low.shape[1] // 2
    idx = idx_ref[...]
    parts = [jnp.where(idx == s, low, jnp.zeros_like(low)) for s in range(slots)]
    for kind, (mine, got) in enumerate([(part_k, got_k), (part_v, got_vv)]):
        for j in range(PIECES // 2):
            total = mine[PIECES // 2 + j] + got[j]
            for s in range(slots):
                total += dot(
                    parts[s][:, kind * rank : (kind + 1) * rank],
                    up[s, kind, :, j * tile : (j + 1) * tile],
                )
            start = kind * width + j * tile
            fresh[:, start : start + tile] = total.astype(BF16)

    rows = QUERY_GROUP * steps_t * NB
    near = 128 // (heads * context)
    old_lanes = context * NB
    new_lanes = steps_t * NB
    factor = HEAD_SIZE ** (-0.5)
    dims = (((1,), (1,)), ((), ()))
    loads[4].wait()

    def weigh(b, carry):
        here = pl.ds(pl.multiple_of(b * NB, NB), NB)
        row, lane = iota((rows, old_lanes), 0), iota((rows, old_lanes), 1)
        live = jnp.concatenate([len_ref[here, :]] * (QUERY_GROUP * steps_t), axis=0)
        old_ok = (row % NB == lane % NB) & (lane // NB < live)
        row, lane = iota((rows, new_lanes), 0), iota((rows, new_lanes), 1)
        new_ok = (row % NB == lane % NB) & (lane // NB <= (row // NB) % steps_t)
        q = query[:, here, :].reshape(steps_t * NB, query.shape[2])
        k = keys[here, :]
        new_k = jnp.concatenate(
            [
                fresh[pl.ds(pl.multiple_of(t * requests + b * NB, NB), NB), :width]
                for t in range(steps_t)
            ],
            axis=0,
        )
        total = jnp.zeros((rows, 128), F32)
        total_new = jnp.zeros((rows, 128), F32)
        row, lane = iota((rows, 128), 0) // NB, iota((rows, 128), 1)
        fold_old = iota((old_lanes, 128), 1) % context == iota((old_lanes, 128), 0) // NB
        fold_old = fold_old.astype(BF16)
        fold_new = iota((new_lanes, 128), 1) % steps_t == iota((new_lanes, 128), 0) // NB
        fold_new = fold_new.astype(BF16)
        for g in range(heads):
            start = g * QUERY_GROUP * HEAD_SIZE
            qg = jnp.concatenate(
                [q[:, start + h * HEAD_SIZE : start + (h + 1) * HEAD_SIZE] for h in range(QUERY_GROUP)],
                axis=0,
            )
            at = g * HEAD_SIZE
            kg = jnp.concatenate(
                [k[:, p * width + at : p * width + at + HEAD_SIZE] for p in range(context)], axis=0
            )
            ng = new_k[:, at : at + HEAD_SIZE]
            old = lax.dot_general(qg, kg, dims, preferred_element_type=F32) * factor
            new = lax.dot_general(qg, ng, dims, preferred_element_type=F32) * factor
            old = jnp.where(old_ok, old, -jnp.inf)
            new = jnp.where(new_ok, new, -jnp.inf)
            top = jnp.maximum(
                jnp.max(old, axis=1, keepdims=True), jnp.max(new, axis=1, keepdims=True)
            )
            old = jnp.exp(old - top)
            new = jnp.exp(new - top)
            norm = jnp.sum(old, axis=1, keepdims=True) + jnp.sum(new, axis=1, keepdims=True)
            scale = 1.0 / norm
            old = (old * scale).astype(BF16)
            new = (new * scale).astype(BF16)
            here_old = lane // context == (row // steps_t) % near * heads + g
            total = jnp.where(here_old, dot(old, fold_old), total)
            total_new = jnp.where(lane // steps_t == row * heads + g, dot(new, fold_new), total_new)
        tiles = QUERY_GROUP // near * steps_t
        for i in range(tiles):
            first = i // steps_t * near * steps_t + i % steps_t
            piece = [total[j * NB : (j + 1) * NB] for j in range(first, first + near * steps_t, steps_t)]
            wts[here, i * 128 : (i + 1) * 128] = sum(piece[1:], piece[0]).astype(BF16)
        piece = [total_new[j * NB : (j + 1) * NB] for j in range(QUERY_GROUP * steps_t)]
        wts[here, tiles * 128 : (tiles + 1) * 128] = sum(piece[1:], piece[0]).astype(BF16)
        return carry

    lax.fori_loop(0, requests // NB, weigh, 0)

    chunk = 2 * width
    for t in range(steps_t):
        place(
            fresh[t * requests : (t + 1) * requests, :], sent_s, slice(t * chunk, (t + 1) * chunk)
        )
    place(wts[...], sent_s, slice(steps_t * chunk, steps_t * chunk + wts.shape[1]))
    send(1)

    rows = QUERY_GROUP * steps_t * SEG
    lanes = (context + steps_t) * SEG

    def serve(v_ref, s_ref, source):
        own = iota((rows, lanes), 0) % SEG == iota((rows, lanes), 1) % SEG
        r, c = iota((256, lanes), 0), iota((256, lanes), 1) // SEG
        spread = ((r < 128) & (r % context == c)) | ((r >= 128) & (context + r % steps_t == c))
        spread = spread.astype(BF16)
        row, lane = iota((rows, 128), 0) // SEG, iota((rows, 128), 1)
        old_at = lane // context - (row // steps_t) % near * heads
        new_at = lane // steps_t - row * heads
        v = v_ref[source].astype(F32)
        s = s_ref[source].astype(F32)
        w = [
            s[:, steps_t * chunk + i * 128 : steps_t * chunk + (i + 1) * 128]
            for i in range(QUERY_GROUP // near * steps_t + 1)
        ]
        w_old = [
            w[h // near * steps_t + t] for h in range(QUERY_GROUP) for t in range(steps_t)
        ]
        w_old = jnp.concatenate(w_old, axis=0)
        w_new = jnp.concatenate([w[-1]] * (QUERY_GROUP * steps_t), axis=0)
        r2, c2 = iota((2 * SEG, 2 * SEG), 0), iota((2 * SEG, 2 * SEG), 1)
        weave = (c2 == (r2 % 2) * SEG + r2 // 2).astype(BF16)
        for t in range(steps_t):
            both = [s[:, t * chunk + i * width : t * chunk + (i + 1) * width] for i in range(2)]
            both = dot(weave, jnp.concatenate(both, axis=0).astype(BF16))
            kv_ref[t, source] = both.reshape(SEG, 2, width).astype(BF16)
        for g in range(heads):
            at = g * HEAD_SIZE
            vg = [v[:, p * width + at : p * width + at + HEAD_SIZE] for p in range(context)]
            for t in range(steps_t):
                start = t * chunk + width + at
                vg.append(s[:, start : start + HEAD_SIZE])
            vg = jnp.concatenate(vg, axis=0).astype(BF16)
            mine = [jnp.where(old_at == g, w_old, 0.0), jnp.where(new_at == g, w_new, 0.0)]
            wide = dot(jnp.concatenate(mine, axis=1).astype(BF16), spread)
            wide = jnp.where(own, wide, 0.0).astype(BF16)
            res = dot(wide, vg)
            for h in range(QUERY_GROUP):
                start = (g * QUERY_GROUP + h) * HEAD_SIZE
                for t in range(steps_t):
                    at_row = (h * steps_t + t) * SEG
                    out_ref[t, source, :, start : start + HEAD_SIZE] = res[
                        at_row : at_row + SEG
                    ].astype(BF16)

    serve(sent_v, sent_s, me)

    def arrive(k):
        incoming(0, k).wait_recv()
        incoming(1, k).wait_recv()
        serve(got_v, got_s, partner(k))

    def step(k, carry):
        arrive(k)
        return carry

    lax.fori_loop(1, n, step, 0)
    for i in range(2):
        for k in range(1, n):
            outgoing(i, k).wait_send()


def on_device(
    tokens,
    queries,
    key_value_cache,
    key_value_length,
    request_adapter_index,
    adapter_destination,
    key_matrix,
    value_matrix,
    adapter_down_maps,
    adapter_up_maps,
):
    slots, depth, rank = adapter_down_maps.shape
    requests = request_adapter_index.shape[0]
    steps_t = tokens.shape[0]
    rows = steps_t * requests
    _, context, _, width = key_value_cache.shape
    query_width = queries.shape[2]
    n = lax.axis_size("inst")
    packed = QUERY_GROUP * steps_t * (width // HEAD_SIZE) * (context + steps_t)
    second = steps_t * 2 * width + packed
    tile = key_matrix.shape[1] // PIECES
    vmem = pl.BlockSpec(memory_space=pltpu.VMEM)
    hbm = pl.BlockSpec(memory_space=pltpu.MemorySpace.HBM)
    dma = pltpu.SemaphoreType.DMA
    attended, new_kv = pl.pallas_call(
        functools.partial(kernel, n, steps_t),
        in_specs=[pl.BlockSpec(memory_space=pltpu.SMEM)] + [vmem] * 2 + [hbm] * 7,
        out_specs=[vmem, vmem],
        out_shape=[
            jax.ShapeDtypeStruct((steps_t, n, SEG, query_width), BF16),
            jax.ShapeDtypeStruct((steps_t, n, SEG, 2, width), BF16),
        ],
        scratch_shapes=[
            pltpu.VMEM(key_value_cache.shape, BF16),
            pltpu.VMEM((rows, depth), BF16),
            pltpu.VMEM((PIECES, depth, tile), BF16),
            pltpu.VMEM((PIECES, depth, tile), BF16),
            pltpu.VMEM(adapter_down_maps.shape, BF16),
            pltpu.VMEM(adapter_up_maps.shape, BF16),
            pltpu.VMEM(queries.shape, BF16),
            pltpu.VMEM((n * SEG, requests), BF16),
            pltpu.VMEM((requests, context * width), BF16),
            pltpu.VMEM((requests, context * width), BF16),
            pltpu.VMEM((n, SEG, context * width), BF16),
            pltpu.VMEM((n, SEG, context * width), BF16),
            pltpu.VMEM((n, SEG, second), BF16),
            pltpu.VMEM((n, SEG, second), BF16),
            pltpu.VMEM((PIECES, rows, tile), F32),
            pltpu.VMEM((PIECES, rows, tile), F32),
            pltpu.VMEM((PIECES // 2, rows, tile), F32),
            pltpu.VMEM((PIECES // 2, rows, tile), F32),
            pltpu.VMEM((rows, rank), F32),
            pltpu.VMEM((rows, rank), F32),
            pltpu.VMEM((rows, 2 * width), BF16),
            pltpu.VMEM((requests, packed), BF16),
            pltpu.VMEM((rows, 1), jnp.int32),
            pltpu.VMEM((requests, 1), jnp.int32),
            dma((5,)),
            dma((2, PIECES)),
            dma((3,)),
            dma((3,)),
            dma((2, n)),
            dma((2, n)),
        ],
        compiler_params=pltpu.CompilerParams(
            collective_id=0, has_side_effects=True, vmem_limit_bytes=(32 + n) * MIB
        ),
        name="migrate",
    )(
        adapter_destination, request_adapter_index.reshape(1, requests),
        key_value_length.reshape(1, requests), key_value_cache, tokens.reshape(rows, depth), key_matrix, value_matrix,
        adapter_down_maps, adapter_up_maps, queries,
    )
    if n != slots:
        coming = adapter_destination.reshape(n, slots) == lax.axis_index("inst")
        coming = jnp.sum(coming.astype(jnp.int32), axis=1)
        hit = coming[None, :] * (jnp.cumsum(coming)[None, :] - 1 == jnp.arange(slots)[:, None])
        anchor = jnp.sum(hit * jnp.arange(n)[None, :], axis=1)
        attended = jnp.take(attended, anchor, axis=1)
        new_kv = jnp.take(new_kv, anchor, axis=1)
    return (
        attended.reshape(steps_t, slots * SEG, query_width),
        new_kv.reshape(steps_t, slots * SEG, 2, width),
    )


def solution(mesh):
    return jax.shard_map(
        on_device,
        mesh=mesh,
        in_specs=(
            P(None, ("grp", "inst"), "tp"),
            P(None, ("grp", "inst"), "tp"),
            P(("grp", "inst"), None, None, "tp"),
            P(("grp", "inst")),
            P(("grp", "inst"), None),
            P("grp"),
            P("tp", None),
            P("tp", None),
            P(("grp", "inst"), "tp", None),
            P(("grp", "inst"), None, None, "tp"),
        ),
        out_specs=(P(None, ("grp", "inst"), "tp"), P(None, ("grp", "inst"), None, "tp")),
        check_vma=False,
    )
```
